256 devices in a mesh: dp: 8 (over x, y_lo), ctx: 32 (over y_hi, z, core).
Axes of the slice: x: 4, y: 4 (y_hi: 2, y_lo: 2; y = y_hi * 2 + y_lo), z: 8, core: 2. Of those that a mesh axis runs over, the one named last changes fastest.
Arguments:
- sequence: bfloat16 [8, 8192, 2048], P('dp', 'ctx'), may hold values from -6 to 6
- n_blocks: int32 [8, 64], P('dp', 'ctx'), may hold values 0 or 1
- w_dt: float32 [2048, 32], replicated, may hold values from -0.125 to 0.125
- dt_bias: float32 [32], replicated, may hold values from -4 to -1
- decay_rate: float32 [32], replicated, may hold values from 2e-05 to 1
- w_b: float32 [2048, 64], replicated, may hold values from -0.015625 to 0.015625
- w_c: float32 [2048, 64], replicated, may hold values from -0.015625 to 0.015625
- d_skip: float32 [32], replicated, may hold values from 0.5 to 1.5
- cotangent: bfloat16 [8, 8192, 2048], P('dp', 'ctx'), may hold values from -6 to 6
Outputs:
- mixed: bfloat16 [8, 8192, 2048], P('dp', 'ctx')
- grad_sequence: bfloat16 [8, 8192, 2048], P('dp', 'ctx')
- grad_w_dt: float32 [2048, 32], replicated
- grad_dt_bias: float32 [32], replicated
- grad_decay_rate: float32 [32], replicated
- grad_w_b: float32 [2048, 64], replicated
- grad_w_c: float32 [2048, 64], replicated
- grad_d_skip: float32 [32], replicated
The draws below stay inside these ranges and needn't reach their ends.
All inputs are finite; a program needn't handle non-finite values. No bound on the sum of `n_blocks` on one device may be relied on, other than what follows from the above.
Results may differ from the reference program's by a relative error of at most 0.001.
Values sent between devices are 32-bit elements; how exact they have to be, the bound alone decides.
A program may use at most 256 MiB of HBM per device.

```python
import math
import jax
import jax.numpy as jnp
from jax import lax

D = 2048
N = 64
BLOCK = 128
H = 32
SEQS = 8
LENGTH = 8192


def plant(drawn, key, smallest, high):
    place = [jax.random.randint(jax.random.fold_in(key, axis), (), 0, length) for axis, length in enumerate(drawn.shape)]
    longest = drawn.shape.index(max(drawn.shape))
    neighbour = place[:longest] + [(place[longest] + 1) % drawn.shape[longest]] + place[longest + 1:]
    return drawn.at[tuple(place)].set(smallest).at[tuple(neighbour)].set(high)


def block_scale(stream_key, dims, split, smallest, high):
    loudness = 1.0
    for position, shards_of in split:
        draws = jax.random.uniform(jax.random.fold_in(jax.random.fold_in(stream_key, 6), position), (shards_of,), jnp.float32, smallest / len(split), high / len(split))
        loudness = loudness * jnp.repeat(jnp.exp(draws), dims[position] // shards_of).reshape((-1,) + (1,) * (len(dims) - 1 - position))
    return loudness


def bell_draw(rng, dims, scale, limit, pieces=(), kind=jnp.bfloat16):
    level = block_scale(rng, dims, pieces, -0.22, 0.18) if pieces else 1.0
    array = jax.random.normal(rng, dims, jnp.float32) * scale * level
    return jnp.minimum(jnp.maximum(array, -limit), limit).astype(kind)


def setup_inputs(seed: int = 0) -> dict:
    key_list = jax.random.split(jax.random.key(seed), 10)
    return {
        "sequence": bell_draw(key_list[0], (SEQS, LENGTH, D), 1.0, 6.0, ((0, 8), (1, 32))),
        "n_blocks": plant((jax.random.randint(key_list[1], (SEQS, LENGTH // BLOCK), 0, 4) < 1).astype(jnp.int32), jax.random.fold_in(key_list[1], 1), 0, 1),
        "w_dt": bell_draw(key_list[2], (D, H), D ** -0.5, 0.125, (), jnp.float32),
        "dt_bias": jnp.clip(jax.random.uniform(key_list[3], (H,), jnp.float32, -4.0, -1.0), -4.0, -1.0),
        "decay_rate": jnp.clip(jnp.exp(jax.random.uniform(key_list[4], (H,), jnp.float32, math.log(1.9999999494757503e-05), math.log(1.0))), 1.9999999494757503e-05, 1.0),
        "w_b": bell_draw(key_list[5], (D, N), (D * N) ** -0.5, 0.015625, (), jnp.float32),
        "w_c": bell_draw(key_list[6], (D, N), (D * N) ** -0.5, 0.015625, (), jnp.float32),
        "d_skip": jnp.clip(jax.random.uniform(key_list[7], (H,), jnp.float32, 0.5, 1.5), 0.5, 1.5),
        "cotangent": bell_draw(key_list[8], (SEQS, LENGTH, D), 1.0, 6.0, ((0, 8), (1, 32))),
    }


precise = lax.Precision.HIGHEST

def strand_pieces(values, keep, params):
    w_dt, dt_bias, decay_rate, w_b, w_c, d_skip = params
    length, width = values.shape
    heads = w_dt.shape[1]
    state_dim = w_b.shape[1]
    head_size = width // heads
    count = length // BLOCK
    steps = jax.nn.softplus(jnp.dot(values, w_dt, precision=precise) + dt_bias) * keep[:, None]
    b_rows = jnp.dot(values, w_b, precision=precise)
    c_rows = jnp.dot(values, w_c, precision=precise)
    log_decay = -steps * decay_rate
    inputs = (steps[:, :, None] * values.reshape(length, heads, head_size)).reshape(count, BLOCK, heads, head_size)
    within = jnp.cumsum(log_decay.reshape(count, BLOCK, heads), axis=1)
    b_blocks = b_rows.reshape(count, BLOCK, state_dim)
    c_blocks = c_rows.reshape(count, BLOCK, state_dim)
    causal = jnp.arange(BLOCK)[:, None] >= jnp.arange(BLOCK)[None, :]

    def advance(state, block_data):
        cum_k, b_k, c_k, u_k = block_data
        diff = cum_k[:, None, :] - cum_k[None, :, :]
        weights = jnp.exp(jnp.where(causal[:, :, None], diff, -1e+30))
        scores = jnp.dot(c_k, b_k.T, precision=precise)
        inner = jnp.einsum('tsh,shp->thp', scores[:, :, None] * weights, u_k, precision=precise)
        from_state = jnp.exp(cum_k)[:, :, None] * jnp.einsum('tn,hnp->thp', c_k, state, precision=precise)
        tail = jnp.exp(cum_k[-1][None, :] - cum_k)
        new_state = jnp.exp(cum_k[-1])[:, None, None] * state + jnp.einsum('sn,shp->hnp', b_k, tail[:, :, None] * u_k, precision=precise)
        return (new_state, inner + from_state)
    start = jnp.zeros((heads, state_dim, head_size), jnp.float32)
    final, outputs = lax.scan(advance, start, (within, b_blocks, c_blocks, inputs))
    skip = jnp.repeat(d_skip, head_size)
    local_out = outputs.reshape(length, width) + skip[None, :] * values
    return local_out

def layer(values, keep, params):
    forward = strand_pieces(values, keep, params)
    backward = strand_pieces(values[::-1, ::-1], keep[::-1], params)
    return forward + backward[::-1, ::-1]

def reference(sequence, n_blocks, w_dt, dt_bias, decay_rate, w_b, w_c, d_skip, cotangent):
    params = (w_dt, dt_bias, decay_rate, w_b, w_c, d_skip)

    def single(item):
        seq_row, block_row, cot_row = item
        values = seq_row.astype(jnp.float32)
        keep = jnp.repeat(1.0 - block_row.astype(jnp.float32), BLOCK)

        def apply_layer(inputs, weights):
            return layer(inputs, keep, weights)
        result, pull = jax.vjp(apply_layer, values, params)
        grad_values, grad_params = pull(cot_row.astype(jnp.float32))
        return (result.astype(jnp.bfloat16), grad_values.astype(jnp.bfloat16), grad_params)
    outputs, grads, grad_params = lax.map(single, (sequence, n_blocks, cotangent))
    summed = [lax.optimization_barrier(jnp.sum(entry, axis=0)) for entry in grad_params]
    return (outputs, grads, summed[0], summed[1], summed[2], summed[3], summed[4], summed[5])
```

```python
import functools

import jax
import jax.numpy as jnp
from jax import lax
from jax.experimental import pallas as pl
from jax.experimental.pallas import tpu as pltpu
from jax.sharding import PartitionSpec as P

F32 = jnp.float32
BF16 = jnp.bfloat16
BLOCK = 128
T = 256
D = 2048
H = 32
N = 64
G = 16
MESH = pl.DeviceIdType.MESH
VMEM = pl.BlockSpec(memory_space=pltpu.VMEM)
SMEM = pl.BlockSpec(memory_space=pltpu.SMEM)
LIMIT = 48 * 1024 * 1024
RATIO = 3
FAR = -1e30


def iota(shape, axis):
    return lax.broadcasted_iota(jnp.int32, shape, axis)


def mat(a, b):
    return lax.dot_general(a, b, (((1,), (0,)), ((), ())), preferred_element_type=F32)


def mat_nt(a, b):
    return lax.dot_general(a, b, (((1,), (1,)), ((), ())), preferred_element_type=F32)


def split2(a):
    hi = a.astype(BF16)
    return hi, (a - hi.astype(F32)).astype(BF16)


def split3(a):
    hi = a.astype(BF16)
    rest = a - hi.astype(F32)
    mid = rest.astype(BF16)
    return hi, mid, (rest - mid.astype(F32)).astype(BF16)


def mat2(a, exact):
    hi, lo = split2(a)
    return mat(hi, exact) + mat(lo, exact)


def mat3(a, b):
    ah, al = split2(a)
    bh, bl = split2(b)
    return mat(ah, bh) + (mat(al, bh) + mat(ah, bl))


def mat3_nt(a, b):
    ah, al = split2(a)
    bh, bl = split2(b)
    return mat_nt(ah, bh) + (mat_nt(al, bh) + mat_nt(ah, bl))


def exact_left(zero_one, a):
    hi, mid, lo = split3(a)
    return mat(zero_one, hi) + (mat(zero_one, mid) + mat(zero_one, lo))


def exact_right(a, zero_one):
    hi, mid, lo = split3(a)
    return mat(hi, zero_one) + (mat(mid, zero_one) + mat(lo, zero_one))


def ones_where(condition):
    return jnp.where(condition, 1.0, 0.0).astype(BF16)


def flip_rows():
    return ones_where(iota((128, 128), 0) + iota((128, 128), 1) == 127)


def keep_column(nb_ref):
    first = 1.0 - nb_ref[0, 0].astype(F32)
    second = 1.0 - nb_ref[0, 1].astype(F32)
    return jnp.where(iota((T, 1), 0) < BLOCK, first, second)


def spread(j, width):
    rows = iota((128, 2 * width), 0)
    cols = iota((128, 2 * width), 1)
    head = j * (width // N) + (cols % width) // N
    return ones_where(rows == head + jnp.where(cols < width, 0, H))


def front_kernel(x_ref, dy_ref, nb_ref, wdt_ref, wb_ref, wc_ref, prm_ref,
                 pack_ref, c_ref, step_ref, z_ref, at_ref, bcf_ref, bcr_ref, whi_ref, wlo_ref):
    flip = flip_rows()
    pick = iota((128, 128), 0)
    cols = iota((128, 128), 1)
    swap = ones_where((pick < H) & (pick + cols == 2 * H - 1))

    def cut(i, carry):
        rows = pl.ds(pl.multiple_of(i * 128, 128), 128)
        dt = jnp.concatenate([wdt_ref[rows, :], jnp.zeros((128, 96), F32)], axis=1)
        bc = jnp.concatenate([wb_ref[rows, :], wc_ref[rows, :]], axis=1)
        dt_hi, dt_lo = split2(dt)
        bc_hi, bc_lo = split2(bc)
        whi_ref[rows, 0:128] = dt_hi
        wlo_ref[rows, 0:128] = dt_lo
        whi_ref[rows, 128:256] = bc_hi
        wlo_ref[rows, 128:256] = bc_lo
        return carry

    lax.fori_loop(0, G, cut, 0)

    def turned(ref, i):
        rows = pl.ds(pl.multiple_of((G - 1 - i) * 128, 128), 128)
        return mat(flip, ref[rows, 0:256]).astype(BF16)

    def mirror(i, carry):
        for ref in (whi_ref, wlo_ref):
            low = pl.ds(pl.multiple_of(i * 128, 128), 128)
            high = pl.ds(pl.multiple_of((G - 1 - i) * 128, 128), 128)
            for_low = turned(ref, i)
            for_high = turned(ref, G - 1 - i)
            for rows, got in ((low, for_low), (high, for_high)):
                ref[rows, 256:384] = got[:, 128:256]
                ref[rows, 0:128] = (
                    ref[rows, 0:128].astype(F32) + mat(got[:, 0:128], swap)
                ).astype(BF16)
        return carry

    lax.fori_loop(0, G // 2, mirror, 0)

    x = x_ref[...]
    proj = mat(x, whi_ref[...]) + mat(x, wlo_ref[...])
    lane = iota((T, 128), 1)
    z = proj[:, 0:128] + prm_ref[0:1, :]
    soft = jnp.maximum(z, 0.0) + jnp.log1p(jnp.exp(-jnp.abs(z)))
    step = jnp.where(lane < 2 * H, soft * keep_column(nb_ref), 0.0)
    fall = -step * prm_ref[1:2, :]
    row = iota((T, T), 0)
    col = iota((T, T), 1)
    c = jnp.where(
        lane < H,
        exact_left(ones_where(row >= col), fall),
        exact_left(ones_where(row <= col), fall),
    )
    last = jnp.where(lane[0:1] < H, c[T - 1 : T], c[0:1])
    a = jnp.where(step > 0.0, jnp.log(jnp.maximum(step, 1e-37)) - c, FAR)
    z_ref[...] = z
    step_ref[...] = step
    c_ref[...] = c
    at_ref[...] = a.T
    bcf = proj[:, 128:256]
    bcr = proj[:, 256:384]
    bcf_ref[...] = bcf
    bcr_ref[...] = bcr

    e2 = jnp.concatenate(split2(jnp.exp(c)), axis=1)
    tail2 = jnp.concatenate(split2(jnp.exp(last - c) * step), axis=1)
    decay = jnp.exp(last)
    decay8 = jnp.broadcast_to(decay, (8, 128))
    tf_hi, tf_lo = split2(bcf.T)
    tr_hi, tr_lo = split2(bcr.T)
    both = [
        jnp.concatenate([hi[s], lo[s]], axis=0)
        for hi, lo, s in (
            (tf_hi, tf_lo, slice(0, N)),
            (tr_hi, tr_lo, slice(N, 2 * N)),
            (tr_hi, tr_lo, slice(0, N)),
            (tf_hi, tf_lo, slice(N, 2 * N)),
        )
    ]

    def states(j, carry):
        cols = pl.ds(pl.multiple_of(j * 128, 128), 128)
        sel = spread(j, 128)
        sel2 = jnp.concatenate([sel, sel], axis=0)
        ee = mat(e2, sel2)
        tt = mat(tail2, sel2)
        dd = exact_right(decay8, sel)
        xj = x_ref[:, cols].astype(F32)
        dj = dy_ref[:, cols].astype(F32)
        right = (tt[:, 0:128] * xj, ee[:, 128:256] * dj, tt[:, 128:256] * xj, ee[:, 0:128] * dj)
        drop = (dd[:, 0:128], dd[:, 128:256], dd[:, 128:256], dd[:, 0:128])
        half = j // 8
        part = j % 8
        for s in range(4):
            hi, lo = split2(right[s])
            wide = mat(both[s], hi)
            pack_ref[half, s, part, 0:N, :] = wide[0:N] + wide[N : 2 * N] + mat(both[s][0:N], lo)
            pack_ref[half, s, part, N : N + 8, :] = drop[s]
        return carry

    lax.fori_loop(0, G, states, 0)


def carry_kernel(chips, pack_ref, out_ref, other, total, drop, came, stage, give,
                 sem_a, sem_b, sem_c, sem_d, sem_e, sem_f):
    dp = lax.axis_index("dp")
    ctx = lax.axis_index("ctx")
    core = ctx % 2
    chip = ctx // 2
    partner = (dp, ctx + 1 - 2 * core)
    after = (dp, jnp.minimum(ctx + 2, 2 * chips - 2 + core))
    before = (dp, jnp.maximum(ctx - 2, core))

    barrier = pltpu.get_barrier_semaphore()
    pl.semaphore_signal(barrier, inc=1, device_id=partner, device_id_type=MESH)

    @pl.when(chip < chips - 1)
    def _():
        pl.semaphore_signal(barrier, inc=1, device_id=after, device_id_type=MESH)

    @pl.when(chip > 0)
    def _():
        pl.semaphore_signal(barrier, inc=1, device_id=before, device_id_type=MESH)

    peers = 1 + (chip < chips - 1).astype(jnp.int32) + (chip > 0).astype(jnp.int32)
    pl.semaphore_wait(barrier, peers)

    def swap(s):
        return pltpu.make_async_remote_copy(
            src_ref=pack_ref.at[1 - core, s], dst_ref=other.at[s],
            send_sem=sem_a.at[s], recv_sem=sem_b.at[s],
            device_id=partner, device_id_type=MESH,
        )

    for s in range(4):
        swap(s).start()

    @pl.when(chip == 0)
    def _():
        came[0:16] = jnp.zeros((16, N, 128), F32)

    @pl.when(chip == chips - 1)
    def _():
        came[16:32] = jnp.zeros((16, N, 128), F32)

    for s in range(4):
        swap(s).wait_recv()
    for s in range(4):
        first = core == (0 if s < 2 else 1)

        def sums(g, carry, s=s, first=first):
            mine = pack_ref[core, s, g, 0:N, :]
            theirs = other[s, g, 0:N, :]
            dm = pack_ref[core, s, g, N : N + 1, :]
            dt = other[s, g, N : N + 1, :]
            total[8 * s + g] = jnp.where(first, dt * mine + theirs, dm * theirs + mine)
            drop[8 * s + g] = jnp.broadcast_to(dm * dt, (8, 128))
            return carry

        lax.fori_loop(0, 8, sums, 0)

    def hop(i, target):
        return pltpu.make_async_remote_copy(
            src_ref=stage.at[i], dst_ref=came.at[i],
            send_sem=sem_c.at[i], recv_sem=sem_d.at[i],
            device_id=target, device_id_type=MESH,
        )

    def hand(i):
        return pltpu.make_async_remote_copy(
            src_ref=give.at[i], dst_ref=out_ref.at[core, i // 8, i % 8],
            send_sem=sem_e.at[i], recv_sem=sem_f.at[i],
            device_id=partner, device_id_type=MESH,
        )

    def piece(i, has_prev, has_next, target, first):
        @pl.when(has_prev)
        def _():
            hop(i, target).wait_recv()

        got = came[i]

        @pl.when(has_next)
        def _():
            stage[i] = drop[i, 0:1, :] * got + total[i]
            hop(i, target).start()

        s = i // 8
        g = i % 8
        mine = pack_ref[core, s, g, 0:N, :]
        theirs = other[s, g, 0:N, :]
        dm = pack_ref[core, s, g, N : N + 1, :]
        dt = other[s, g, N : N + 1, :]
        out_ref[core, s, g] = jnp.where(first, got, dt * got + theirs)
        give[i] = jnp.where(first, dm * got + mine, got)
        hand(i).start()

    def turn(tau, carry):
        up = tau - RATIO * chip
        down = tau - RATIO * (chips - 1 - chip)

        @pl.when((up >= 0) & (up < 16))
        def _():
            piece(up, chip > 0, chip < chips - 1, after, core == 0)

        @pl.when((down >= 0) & (down < 16))
        def _():
            piece(16 + down, chip < chips - 1, chip > 0, before, core == 1)

        return carry

    lax.fori_loop(0, RATIO * (chips - 1) + 16, turn, 0)

    def finish(i, carry):
        pltpu.make_async_remote_copy(
            src_ref=give.at[i], dst_ref=out_ref.at[1 - core, i // 8, i % 8],
            send_sem=sem_e.at[i], recv_sem=sem_f.at[i],
            device_id=partner, device_id_type=MESH,
        ).wait_recv()
        hand(i).wait_send()
        return carry

    lax.fori_loop(0, 32, finish, 0)

    @pl.when(chip < chips - 1)
    def _():
        def sent(i, carry):
            hop(i, after).wait_send()
            return carry

        lax.fori_loop(0, 16, sent, 0)

    @pl.when(chip > 0)
    def _():
        def sent(i, carry):
            hop(i, before).wait_send()
            return carry

        lax.fori_loop(16, 32, sent, 0)

    for s in range(4):
        swap(s).wait_send()


def inner_setup(c_ref, bcf_ref, bcr_ref, sc, c3, dsc):
    bcf = bcf_ref[...]
    bcr = bcr_ref[...]
    row = iota((T, T), 0)
    col = iota((T, T), 1)
    sf = mat3_nt(bcf[:, N:], bcf[:, :N])
    sr = mat3_nt(bcr[:, N:], bcr[:, :N])
    sc[...] = jnp.where(row > col, sf, jnp.where(row < col, sr, 0.0))
    c3[...] = jnp.concatenate(split3(c_ref[...]), axis=1)
    dsc[...] = jnp.zeros((T, T), F32)


def inner_pair(i, x_ref, dy_ref, at_ref, sc, c3, y_ref, dx_ref, dsc, rs_ref, cs_ref):
    cols = pl.ds(pl.multiple_of(i * 128, 128), 128)
    xp = x_ref[:, cols]
    dp = dy_ref[:, cols]
    dpt = dp.astype(F32).T.astype(BF16)
    lane = iota((1, 128), 1)
    row = iota((BLOCK, BLOCK), 0)
    col = iota((BLOCK, BLOCK), 1)
    low = row > col
    up = row < col
    lanes = iota((T, 128), 1)
    y = jnp.zeros((T, 128), F32)
    dut = []
    for k in range(2):
        h = 2 * i + k
        mask = ones_where((lane // N) == k)
        xm = xp * mask
        cross = mat_nt(dp * mask, xp)
        rows3 = iota((384, T), 0) % 128
        cols3 = iota((384, T), 1)
        sel = ones_where(rows3 == h + jnp.where(cols3 < 128, 0, H))
        cb = mat(c3[...], sel)
        af = at_ref[pl.ds(h, 1), :]
        ar = at_ref[pl.ds(H + h, 1), :]
        top = slice(0, BLOCK)
        bot = slice(BLOCK, T)

        def args(rows, columns):
            forward = cb[rows, 0:128] + af[:, columns]
            reverse = cb[rows, 128:256] + ar[:, columns]
            return forward, reverse

        e = {}
        for r in (top, bot):
            for q in (top, bot):
                f, b = args(r, q)
                if r is q:
                    arg = jnp.where(low, f, jnp.where(up, b, FAR))
                else:
                    arg = f if r is bot else b
                e[r is bot, q is bot] = jnp.exp(arg)
        kk = {}
        g = {}
        for r in (top, bot):
            for q in (top, bot):
                key = (r is bot, q is bot)
                kk[key] = sc[r, q] * e[key]
                xx = cross[r, q]
                g[key] = xx * kk[key]
                dsc[r, q] += xx * e[key]
        g0f = jnp.where(low, g[False, False], 0.0)
        g0r = g[False, False] - g0f
        g1f = jnp.where(low, g[True, True], 0.0)
        g1r = g[True, True] - g1f
        rf = jnp.concatenate(
            [jnp.sum(g0f, axis=1, keepdims=True),
             jnp.sum(g[True, False] + g1f, axis=1, keepdims=True)], axis=0)
        rr = jnp.concatenate(
            [jnp.sum(g0r + g[False, True], axis=1, keepdims=True),
             jnp.sum(g1r, axis=1, keepdims=True)], axis=0)
        rs_ref[...] = jnp.where(lanes == h, rf, jnp.where(lanes == H + h, rr, rs_ref[...]))
        cs_ref[pl.ds(h, 1), :] = jnp.concatenate(
            [jnp.sum(g0f + g[True, False], axis=0, keepdims=True),
             jnp.sum(g1f, axis=0, keepdims=True)], axis=1)
        cs_ref[pl.ds(H + h, 1), :] = jnp.concatenate(
            [jnp.sum(g0r, axis=0, keepdims=True),
             jnp.sum(g[False, True] + g1r, axis=0, keepdims=True)], axis=1)
        full = jnp.concatenate(
            [jnp.concatenate([kk[False, False], kk[False, True]], axis=1),
             jnp.concatenate([kk[True, False], kk[True, True]], axis=1)], axis=0)
        hi, lo = split2(full)
        y = y + mat(hi, xm) + mat(lo, xm)
        rows = dpt[N * k : N * (k + 1), :]
        dut.append(mat(rows, hi) + mat(rows, lo))
    y_ref[:, cols] = y
    dx_ref[:, cols] = jnp.concatenate(dut, axis=0).T


def inner_kernel(x_ref, dy_ref, c_ref, at_ref, bcf_ref, bcr_ref,
                 y_ref, dx_ref, dsc_ref, rs_ref, cs_ref, sc, c3):
    inner_setup(c_ref, bcf_ref, bcr_ref, sc, c3, dsc_ref)
    rs_ref[...] = jnp.zeros((T, 128), F32)
    cs_ref[...] = jnp.zeros((128, T), F32)

    def one(i, carry):
        inner_pair(i, x_ref, dy_ref, at_ref, sc, c3, y_ref, dx_ref, dsc_ref, rs_ref, cs_ref)
        return carry

    lax.fori_loop(0, G, one, 0)


def back_kernel(x_ref, dy_ref, nb_ref, prm_ref, c_ref, step_ref, z_ref, bcf_ref, bcr_ref,
                whi_ref, wlo_ref, yin_ref, dxin_ref, dsc_ref, rs_ref, cs_ref, car_ref,
                mixed_ref, dseq_ref, grad_ref,
                dx, rho, kap, xi, omega, dcf, dbf, dcr, dbr):
    lane = iota((T, 128), 1)
    c = c_ref[...]
    step = step_ref[...]
    z = z_ref[...]
    bcf = bcf_ref[...]
    bcr = bcr_ref[...]
    last = jnp.where(lane[0:1] < H, c[T - 1 : T], c[0:1])
    e2 = jnp.concatenate(split2(jnp.exp(c)), axis=1)
    tail2 = jnp.concatenate(split2(jnp.exp(last - c) * step), axis=1)
    sig_f = jnp.sum(bcf[:, :N] * bcf[:, N:], axis=1, keepdims=True)
    sig_r = jnp.sum(bcr[:, :N] * bcr[:, N:], axis=1, keepdims=True)
    sigma = jnp.where(lane < H, sig_f, jnp.where(lane < 2 * H, sig_r, 0.0))
    coef3 = jnp.concatenate(split3(sigma * step + prm_ref[2:3, :]), axis=1)
    for ref in (rho, kap, xi):
        ref[...] = jnp.zeros((T, 128), F32)
    omega[...] = jnp.zeros((8, 128), F32)
    for ref in (dcf, dbf, dcr, dbr):
        ref[...] = jnp.zeros((T, N), F32)
    cuts = {"bf": split2(bcf[:, :N]), "cf": split2(bcf[:, N:]),
            "br": split2(bcr[:, :N]), "cr": split2(bcr[:, N:])}

    def times(name, right):
        lh, ll = cuts[name]
        rh, rl = right
        return mat(lh, rh) + (mat(ll, rh) + mat(lh, rl))

    def times_nt(left, right):
        lh, ll = split2(left)
        rh, rl = right
        return mat_nt(lh, rh) + (mat_nt(ll, rh) + mat_nt(lh, rl))

    def group(j, carry):
        cols = pl.ds(pl.multiple_of(j * 128, 128), 128)
        half = j // 8
        part = j % 8
        state_f = car_ref[half, 0, part]
        adj_r = car_ref[half, 1, part]
        state_r = car_ref[half, 2, part]
        adj_f = car_ref[half, 3, part]
        sel = spread(j, 128)
        sel2 = jnp.concatenate([sel, sel], axis=0)
        ee = mat(e2, sel2)
        tt = mat(tail2, sel2)
        one = sel[:, 0:128] + sel[:, 128:256]
        coef = mat(coef3, jnp.concatenate([one, one, one], axis=0))
        xj = x_ref[:, cols].astype(F32)
        dj = dy_ref[:, cols].astype(F32)
        sf2, sr2, af2, ar2 = split2(state_f), split2(state_r), split2(adj_f), split2(adj_r)
        ef, er = ee[:, 0:128], ee[:, 128:256]
        wf, wr = tt[:, 0:128] * xj, tt[:, 128:256] * xj
        yf = ef * times("cf", sf2)
        yr = er * times("cr", sr2)
        vf = times("bf", af2)
        vr = times("br", ar2)
        mixed_ref[:, cols] = (yin_ref[:, cols] + (yf + yr) + coef * xj).astype(BF16)
        dx[:, cols] = (
            dxin_ref[:, cols] + (tt[:, 0:128] * vf + tt[:, 128:256] * vr) + coef * dj
        )
        back = sel.astype(F32).T.astype(BF16)
        rho[...] += mat2(jnp.concatenate([dj * yf, dj * yr], axis=1), back)
        kap[...] += mat2(jnp.concatenate([wf * vf, wr * vr], axis=1), back)
        xi[...] += mat2(dj * xj, back[0:128] + back[128:256])
        inner = jnp.concatenate(
            [jnp.sum(state_f * adj_f, axis=0, keepdims=True),
             jnp.sum(state_r * adj_r, axis=0, keepdims=True)], axis=1)
        omega[...] += exact_right(jnp.broadcast_to(inner, (8, 256)), back)
        dcf[...] += times_nt(ef * dj, sf2)
        dcr[...] += times_nt(er * dj, sr2)
        dbf[...] += times_nt(wf, af2)
        dbr[...] += times_nt(wr, ar2)
        return carry

    lax.fori_loop(0, G, group, 0)

    row = iota((T, T), 0)
    col = iota((T, T), 1)
    colsum = cs_ref[...].T
    kappa = kap[...]
    through = rs_ref[...] - colsum + rho[...]
    ahead = ones_where(row <= col)
    behind = ones_where(row >= col)
    strict_behind = ones_where(row > col)
    strict_ahead = ones_where(row < col)
    d_fall = jnp.where(
        lane < H,
        exact_left(ahead, through) + exact_left(strict_behind, kappa),
        exact_left(behind, through) + exact_left(strict_ahead, kappa),
    ) + omega[0:1, :] * jnp.exp(last)
    small = jnp.exp(-jnp.abs(z))
    soft = jnp.maximum(z, 0.0) + jnp.log1p(small)
    sigmoid = jnp.where(z >= 0.0, 1.0, small) / (1.0 + small)
    ratio = jnp.where(z < -30.0, 1.0, sigmoid / jnp.maximum(soft, 1e-30))
    ksi = xi[...]
    diag = step * ksi
    straight = colsum + kappa + sigma * diag
    dz = straight * ratio - prm_ref[1:2, :] * d_fall * sigmoid * keep_column(nb_ref)
    dz = jnp.where(lane < 2 * H, dz, 0.0)

    ds_f = jnp.sum(jnp.where(lane < H, diag, 0.0), axis=1, keepdims=True)
    ds_r = jnp.sum(jnp.where((lane >= H) & (lane < 2 * H), diag, 0.0), axis=1, keepdims=True)
    dsc = dsc_ref[...]
    turned = dsc.T
    eq = row == col
    m_f = jnp.where(eq, ds_f, jnp.where(row > col, dsc, 0.0))
    m_r = jnp.where(eq, ds_r, jnp.where(row < col, dsc, 0.0))
    mt_f = jnp.where(eq, ds_f, jnp.where(row < col, turned, 0.0))
    mt_r = jnp.where(eq, ds_r, jnp.where(row > col, turned, 0.0))
    d_cf = dcf[...] + mat3(m_f, bcf[:, :N])
    d_bf = dbf[...] + mat3(mt_f, bcf[:, N:])
    d_cr = dcr[...] + mat3(m_r, bcr[:, :N])
    d_br = dbr[...] + mat3(mt_r, bcr[:, N:])
    dproj = jnp.concatenate([dz, d_bf, d_cf, d_br, d_cr], axis=1)
    p_hi, p_lo = split2(dproj)
    p_cat = jnp.concatenate([p_hi, p_lo, p_hi], axis=1)

    r128 = iota((128, 128), 0)
    c128 = iota((128, 128), 1)
    fold = ones_where(((r128 < H) & (r128 == c128))
                      | ((r128 >= H) & (r128 < 2 * H) & (r128 + c128 == 2 * H - 1)))
    vectors = jnp.concatenate(
        [jnp.sum(dz, axis=0, keepdims=True),
         -jnp.sum(step * d_fall, axis=0, keepdims=True),
         jnp.sum(ksi, axis=0, keepdims=True),
         jnp.zeros((5, 128), F32)], axis=0)
    rows_all = grad_ref.shape[0]
    grad_ref[D + D // 4 : rows_all, :] = jnp.zeros((rows_all - D - D // 4, 128), F32)
    grad_ref[D + D // 4 : D + D // 4 + 8, :] = exact_right(vectors, fold)

    rep_f = ones_where((r128 < H) & (r128 == c128 % H))
    rep_r = ones_where((r128 >= H) & (r128 < 2 * H) & (2 * H - 1 - r128 == c128 % H))

    def right_side(part):
        dt_f = mat(part[:, 0:128], rep_f).astype(BF16)
        dt_r = mat(part[:, 0:128], rep_r).astype(BF16)
        return jnp.concatenate(
            [jnp.concatenate([part[:, 128:256], dt_f], axis=1),
             jnp.concatenate([part[:, 256:384], dt_r], axis=1)], axis=0)

    r_hi = right_side(p_hi)
    r_lo = right_side(p_lo)
    flip = flip_rows()

    def final(j, carry):
        cols = pl.ds(pl.multiple_of(j * 128, 128), 128)
        far = pl.ds(pl.multiple_of((G - 1 - j) * 128, 128), 128)
        w_hi = whi_ref[cols, :]
        w_cat = jnp.concatenate([w_hi, w_hi, wlo_ref[cols, :]], axis=1)
        dseq_ref[:, cols] = (dx[:, cols] + mat_nt(p_cat, w_cat)).astype(BF16)
        x_here = x_ref[:, cols].astype(F32).T.astype(BF16)
        x_far = x_ref[:, far].astype(F32).T.astype(BF16)
        left = jnp.concatenate([x_here, mat(flip, x_far).astype(BF16)], axis=1)
        grads = mat(left, r_hi) + mat(left, r_lo)
        grad_ref[cols, :] = grads[:, 0:128]
        spot = pl.ds(pl.multiple_of(D + (j % 4) * 128, 128), 128)
        mine = iota((128, 128), 1) // H == j // 4
        grad_ref[spot, :] = jnp.where(
            mine, grads[:, 128:256], jnp.where(j < 4, 0.0, grad_ref[spot, :]))
        return carry

    lax.fori_loop(0, G, final, 0)


def sum_kernel(halves, depth, g_ref, out_ref, from_core, held, from_plane, part, from_z, full,
               s_core, r_core, s_plane, r_plane, s_z, r_z, s_zg, r_zg, s_pg, r_pg, s_cg, r_cg):
    dp = lax.axis_index("dp")
    ctx = lax.axis_index("ctx")
    plane = g_ref.shape[0] // 2
    tiles = g_ref.shape[1]
    zt = from_z.shape[1]
    core = ctx % 2
    z = (ctx // 2) % depth
    me = dp * halves + ctx // (2 * depth)
    partner = (dp, ctx + 1 - 2 * core)

    def plane_device(k):
        return (k // halves, ((k % halves) * depth + z) * 2 + core)

    def z_device(j):
        return (dp, ((ctx // (2 * depth)) * depth + j) * 2 + core)

    def peer(i):
        return lax.rem(me + 1 + i, plane)

    def z_peer(i):
        return lax.rem(z + 1 + i, depth)

    def remote(src, dst, send, recv, device):
        return pltpu.make_async_remote_copy(
            src_ref=src, dst_ref=dst, send_sem=send, recv_sem=recv,
            device_id=device, device_id_type=MESH,
        )

    def loop(count, body):
        def step(i, carry):
            body(i)
            return carry

        lax.fori_loop(0, count, step, 0)

    barrier = pltpu.get_barrier_semaphore()
    pl.semaphore_signal(barrier, inc=1, device_id=partner, device_id_type=MESH)
    loop(plane - 1, lambda i: pl.semaphore_signal(
        barrier, inc=1, device_id=plane_device(peer(i)), device_id_type=MESH))
    loop(depth - 1, lambda i: pl.semaphore_signal(
        barrier, inc=1, device_id=z_device(z_peer(i)), device_id_type=MESH))
    pl.semaphore_wait(barrier, plane + depth - 1)

    def core_copy(k):
        return remote(g_ref.at[(1 - core) * plane + k], from_core.at[k],
                      s_core.at[k], r_core.at[k], partner)

    def plane_copy(k):
        return remote(held.at[k], from_plane.at[me], s_plane.at[k], r_plane.at[me],
                      plane_device(k))

    loop(plane, lambda i: core_copy(peer(i)).start())

    def add_core(i):
        k = peer(i)
        core_copy(k).wait_recv()
        held[k] = g_ref[core * plane + k] + from_core[k]

    def forward(i):
        add_core(i)
        plane_copy(peer(i)).start()

    loop(plane - 1, forward)
    add_core(plane - 1)
    part[...] = jnp.zeros(part.shape, F32)
    part[0:tiles] = held[me]

    def add_plane(i):
        k = lax.rem(me + plane - 1 - i, plane)
        remote(held.at[k], from_plane.at[k], s_plane.at[k], r_plane.at[k],
               plane_device(k)).wait_recv()
        part[0:tiles] += from_plane[k]

    loop(plane - 1, add_plane)

    def z_copy(j):
        return remote(part.at[pl.ds(j * zt, zt)], from_z.at[z], s_z.at[j], r_z.at[z], z_device(j))

    loop(depth - 1, lambda i: z_copy(z_peer(i)).start())
    full[pl.ds(z * zt, zt)] = part[pl.ds(z * zt, zt)]

    def add_z(i):
        j = z_peer(i)
        remote(part.at[pl.ds(j * zt, zt)], from_z.at[j], s_z.at[j], r_z.at[j],
               z_device(j)).wait_recv()
        full[pl.ds(z * zt, zt)] += from_z[j]

    loop(depth - 1, add_z)

    def z_share(j):
        return remote(full.at[pl.ds(z * zt, zt)], full.at[pl.ds(z * zt, zt)],
                      s_zg.at[j], r_zg.at[z], z_device(j))

    loop(depth - 1, lambda i: z_share(z_peer(i)).start())

    def z_got(i):
        j = z_peer(i)
        remote(full.at[pl.ds(j * zt, zt)], full.at[pl.ds(j * zt, zt)],
               s_zg.at[j], r_zg.at[j], z_device(j)).wait_recv()

    loop(depth - 1, z_got)
    mine = core * plane + me
    out_ref[mine] = full[0:tiles]

    def plane_share(k):
        return remote(out_ref.at[mine], out_ref.at[mine], s_pg.at[k], r_pg.at[me], plane_device(k))

    def core_share(k):
        return remote(out_ref.at[core * plane + k], out_ref.at[core * plane + k],
                      s_cg.at[k], r_cg.at[k], partner)

    loop(plane - 1, lambda i: plane_share(peer(i)).start())
    core_share(me).start()

    def plane_got(i):
        k = lax.rem(me + plane - 1 - i, plane)
        spot = out_ref.at[core * plane + k]
        remote(spot, spot, s_pg.at[k], r_pg.at[k], plane_device(k)).wait_recv()
        core_share(k).start()

    loop(plane - 1, plane_got)

    def core_got(k):
        spot = out_ref.at[(1 - core) * plane + k]
        remote(spot, spot, s_cg.at[k], r_cg.at[k], partner).wait_recv()

    loop(plane, core_got)
    loop(plane, lambda k: core_copy(k).wait_send())
    loop(plane, lambda k: core_share(k).wait_send())
    loop(plane - 1, lambda i: plane_copy(peer(i)).wait_send())
    loop(plane - 1, lambda i: plane_share(peer(i)).wait_send())
    loop(depth - 1, lambda i: z_copy(z_peer(i)).wait_send())
    loop(depth - 1, lambda i: z_share(z_peer(i)).wait_send())


def sds(shape, dtype=F32):
    return jax.ShapeDtypeStruct(shape, dtype)


def local_call(kernel, ins, outs, scratch=()):
    return pl.pallas_call(
        kernel,
        out_shape=outs,
        in_specs=ins,
        out_specs=[VMEM] * len(outs),
        scratch_shapes=list(scratch),
        compiler_params=pltpu.CompilerParams(vmem_limit_bytes=LIMIT),
    )


def on_device(sizes, sequence, n_blocks, w_dt, dt_bias, decay_rate, w_b, w_c, d_skip, cotangent):
    dps, ctxs = sizes
    halves = 2 if ctxs % 4 == 0 else 1
    depth = ctxs // (2 * halves)
    plane = dps * halves
    tiles = -(-((D + D // 4) // 8 + 1) // (2 * plane))
    zt = -(-tiles // depth)
    x = sequence[0]
    dy = cotangent[0]
    prm = jnp.stack([dt_bias, decay_rate, d_skip])
    prm = jnp.pad(jnp.concatenate([prm, prm[:, ::-1]], axis=1), ((0, 5), (0, 64)))

    pack, c, step, z, at, bcf, bcr, whi, wlo = local_call(
        front_kernel,
        [VMEM, VMEM, SMEM, VMEM, VMEM, VMEM, VMEM],
        [sds((2, 4, 8, N + 8, 128)), sds((T, 128)), sds((T, 128)), sds((T, 128)),
         sds((128, T)), sds((T, 128)), sds((T, 128)), sds((D, 384), BF16), sds((D, 384), BF16)],
    )(x, dy, n_blocks, w_dt, w_b, w_c, prm)

    yin, dxin, dsc, rs, cs = local_call(
        inner_kernel,
        [VMEM] * 6,
        [sds((T, D)), sds((T, D)), sds((T, T)), sds((T, 128)), sds((128, T))],
        [pltpu.VMEM((T, T), F32), pltpu.VMEM((T, 384), BF16)],
    )(x, dy, c, at, bcf, bcr)

    dma = pltpu.SemaphoreType.DMA
    carried = pl.pallas_call(
        functools.partial(carry_kernel, ctxs // 2),
        out_shape=sds((2, 4, 8, N, 128)),
        in_specs=[VMEM],
        out_specs=VMEM,
        scratch_shapes=[
            pltpu.VMEM((4, 8, N + 8, 128), F32),
            pltpu.VMEM((32, N, 128), F32),
            pltpu.VMEM((32, 8, 128), F32),
            pltpu.VMEM((32, N, 128), F32),
            pltpu.VMEM((32, N, 128), F32),
            pltpu.VMEM((32, N, 128), F32),
            dma((4,)), dma((4,)), dma((32,)), dma((32,)), dma((32,)), dma((32,)),
        ],
        compiler_params=pltpu.CompilerParams(
            vmem_limit_bytes=LIMIT, collective_id=0, has_side_effects=True),
    )(pack)

    mixed, dseq, grads = local_call(
        back_kernel,
        [VMEM, VMEM, SMEM] + [VMEM] * 14,
        [sds((T, D), BF16), sds((T, D), BF16), sds((2 * plane * tiles * 8, 128))],
        [pltpu.VMEM((T, D), F32)] + [pltpu.VMEM((T, 128), F32)] * 3
        + [pltpu.VMEM((8, 128), F32)] + [pltpu.VMEM((T, N), F32)] * 4,
    )(x, dy, n_blocks, prm, c, step, z, bcf, bcr, whi, wlo, yin, dxin, dsc, rs, cs, carried)

    summed = pl.pallas_call(
        functools.partial(sum_kernel, halves, depth),
        out_shape=sds((2 * plane, tiles, 8, 128)),
        in_specs=[VMEM],
        out_specs=VMEM,
        scratch_shapes=[
            pltpu.VMEM((plane, tiles, 8, 128), F32),
            pltpu.VMEM((plane, tiles, 8, 128), F32),
            pltpu.VMEM((plane, tiles, 8, 128), F32),
            pltpu.VMEM((depth * zt, 8, 128), F32),
            pltpu.VMEM((depth, zt, 8, 128), F32),
            pltpu.VMEM((depth * zt, 8, 128), F32),
            dma((plane,)), dma((plane,)), dma((plane,)), dma((plane,)),
            dma((depth,)), dma((depth,)), dma((depth,)), dma((depth,)),
            dma((plane,)), dma((plane,)), dma((plane,)), dma((plane,)),
        ],
        compiler_params=pltpu.CompilerParams(
            vmem_limit_bytes=LIMIT, collective_id=1, has_side_effects=True),
    )(grads.reshape(2 * plane, tiles, 8, 128)).reshape(-1, 128)

    quarter = D // 4
    grad_dt = jnp.concatenate(
        [summed[D : D + quarter, H * q : H * (q + 1)] for q in range(4)], axis=0)
    vectors = summed[D + quarter : D + quarter + 3, :H]
    return (mixed[None], dseq[None], grad_dt, vectors[0], vectors[1],
            summed[:D, :N], summed[:D, N:], vectors[2])


def solution(mesh):
    sizes = (mesh.shape["dp"], mesh.shape["ctx"])
    return jax.shard_map(
        functools.partial(on_device, sizes),
        mesh=mesh,
        in_specs=(
            P("dp", "ctx", None),
            P("dp", "ctx"),
            P(), P(), P(), P(), P(), P(),
            P("dp", "ctx", None),
        ),
        out_specs=(P("dp", "ctx", None), P("dp", "ctx", None), P(), P(), P(), P(), P(), P()),
        check_vma=False,
    )
```

```python
import functools

import jax
import jax.numpy as jnp
from jax import lax
from jax.experimental import pallas as pl
from jax.experimental.pallas import tpu as pltpu
from jax.sharding import PartitionSpec as P

F32 = jnp.float32
BF16 = jnp.bfloat16
BLOCK = 128
T = 256
D = 2048
H = 32
N = 64
G = 16
W = D // 256
MESH = pl.DeviceIdType.MESH
VMEM = pl.BlockSpec(memory_space=pltpu.VMEM)
SMEM = pl.BlockSpec(memory_space=pltpu.SMEM)
LIMIT = 48 * 1024 * 1024
ALL = 62 * 1024 * 1024
PIECES = 16
ROWS = 4 * 32 + 8
FAR = -1e30


def iota(shape, axis):
    return lax.broadcasted_iota(jnp.int32, shape, axis)


def mat(a, b):
    return lax.dot_general(a, b, (((1,), (0,)), ((), ())), preferred_element_type=F32)


def mat_nt(a, b):
    return lax.dot_general(a, b, (((1,), (1,)), ((), ())), preferred_element_type=F32)


def split2(a):
    hi = a.astype(BF16)
    return hi, (a - hi.astype(F32)).astype(BF16)


def split3(a):
    hi = a.astype(BF16)
    rest = a - hi.astype(F32)
    mid = rest.astype(BF16)
    return hi, mid, (rest - mid.astype(F32)).astype(BF16)


def mat2(a, exact):
    hi, lo = split2(a)
    return mat(hi, exact) + mat(lo, exact)


def mat3(a, b):
    ah, al = split2(a)
    bh, bl = split2(b)
    return mat(ah, bh) + (mat(al, bh) + mat(ah, bl))


def mat3_nt(a, b):
    ah, al = split2(a)
    bh, bl = split2(b)
    return mat_nt(ah, bh) + (mat_nt(al, bh) + mat_nt(ah, bl))


def exact_left(zero_one, a):
    hi, mid, lo = split3(a)
    return mat(zero_one, hi) + (mat(zero_one, mid) + mat(zero_one, lo))


def exact_right(a, zero_one):
    hi, mid, lo = split3(a)
    return mat(hi, zero_one) + (mat(mid, zero_one) + mat(lo, zero_one))


def ones_where(condition):
    return jnp.where(condition, 1.0, 0.0).astype(BF16)


def backwards(size):
    return ones_where(iota((size, size), 0) + iota((size, size), 1) == size - 1)


def keep_column(nb_ref):
    first = 1.0 - nb_ref[0, 0].astype(F32)
    second = 1.0 - nb_ref[0, 1].astype(F32)
    return jnp.where(iota((T, 1), 0) < BLOCK, first, second)


def spread(first, second):
    rows = iota((128, 256), 0)
    cols = iota((128, 256), 1)
    head = jnp.where(cols < 128, 2 * first, 2 * second) + (cols % 128) // N
    return ones_where(rows == head), ones_where(rows == head + H)


def twice(a):
    return jnp.concatenate([a, a], axis=0)


def lanes2(a):
    return jnp.concatenate(split2(a), axis=1)


def front_kernel(x_ref, dy_ref, nb_ref, wdt_ref, wb_ref, wc_ref, bias_ref, rate_ref, skip_ref,
                 pack_ref, prm_ref, c_ref, step_ref, z_ref, at_ref, bcf_ref, bcr_ref,
                 whi_ref, wlo_ref):
    flip = backwards(256)
    rev = backwards(H)
    both = ones_where((iota((H, 128), 1) == iota((H, 128), 0))
                      | (iota((H, 128), 1) + iota((H, 128), 0) == 2 * H - 1))
    for n, ref in enumerate((bias_ref, rate_ref, skip_ref)):
        prm_ref[n : n + 1, :] = exact_right(jnp.broadcast_to(ref[...], (8, H)), both)[0:1]
    prm_ref[3:8, :] = jnp.zeros((5, 128), F32)

    def cut(i, carry):
        here = pl.ds(pl.multiple_of(i * 256, 256), 256)
        there = pl.ds(pl.multiple_of((W - 1 - i) * 256, 256), 256)
        raw = jnp.concatenate([wdt_ref[:, here], wb_ref[:, here], wc_ref[:, here]], axis=0)
        hi, lo = split2(raw)
        turned = mat(jnp.concatenate([hi, lo], axis=0), flip).astype(BF16)
        for ref, own, far in ((whi_ref, hi, turned[0:160]), (wlo_ref, lo, turned[160:320])):
            ref[0:H, here] = own[0:H]
            ref[128:256, here] = own[H:160]
            ref[H : 2 * H, there] = mat(rev, far[0:H]).astype(BF16)
            ref[256:384, there] = far[H:160]
            ref[2 * H : 128, here] = jnp.zeros((2 * H, 256), BF16)
        return carry

    lax.fori_loop(0, W, cut, 0, unroll=2)

    x = x_ref[...]
    proj = mat_nt(x, whi_ref[...]) + mat_nt(x, wlo_ref[...])
    lane = iota((T, 128), 1)
    z = proj[:, 0:128] + prm_ref[0:1, :]
    soft = jnp.maximum(z, 0.0) + jnp.log1p(jnp.exp(-jnp.abs(z)))
    step = jnp.where(lane < 2 * H, soft * keep_column(nb_ref), 0.0)
    fall = -step * prm_ref[1:2, :]
    row = iota((T, T), 0)
    col = iota((T, T), 1)
    c = jnp.where(
        lane < H,
        exact_left(ones_where(row >= col), fall),
        exact_left(ones_where(row <= col), fall),
    )
    last = jnp.where(lane[0:1] < H, c[T - 1 : T], c[0:1])
    a = jnp.where(step > 0.0, jnp.log(jnp.maximum(step, 1e-37)) - c, FAR)
    z_ref[...] = z
    step_ref[...] = step
    c_ref[...] = c
    at_ref[...] = a.T
    bcf = proj[:, 128:256]
    bcr = proj[:, 256:384]
    bcf_ref[...] = bcf
    bcr_ref[...] = bcr

    e2 = lanes2(jnp.exp(c))
    tail2 = lanes2(jnp.exp(last - c) * step)
    decay8 = jnp.broadcast_to(jnp.exp(last), (8, 128))
    tf_hi, tf_lo = split2(bcf.T)
    tr_hi, tr_lo = split2(bcr.T)
    lefts = [
        jnp.concatenate([hi[part], lo[part]], axis=0)
        for hi, lo, part in (
            (tf_hi, tf_lo, slice(0, N)),
            (tr_hi, tr_lo, slice(N, 2 * N)),
            (tr_hi, tr_lo, slice(0, N)),
            (tf_hi, tf_lo, slice(N, 2 * N)),
        )
    ]

    def states(i, carry):
        cols = pl.ds(pl.multiple_of(i * 256, 256), 256)
        sel_f, sel_r = spread(2 * i, 2 * i + 1)
        two_f, two_r = twice(sel_f), twice(sel_r)
        xj = x_ref[:, cols].astype(F32)
        dj = dy_ref[:, cols].astype(F32)
        rights = (mat(tail2, two_f) * xj, mat(e2, two_r) * dj,
                  mat(tail2, two_r) * xj, mat(e2, two_f) * dj)
        dd_f, dd_r = exact_right(decay8, sel_f), exact_right(decay8, sel_r)
        which = iota((8, 256), 0)
        drops = jnp.where((which == 0) | (which == 3), dd_f, dd_r)
        half = i // (W // 2)
        for s in range(4):
            hi, lo = split2(rights[s])
            wide = mat(lefts[s], hi)
            got = wide[0:N] + wide[N : 2 * N] + mat(lefts[s][0:N], lo)
            for g in range(2):
                for r in range(2):
                    piece = 4 * (i % (W // 2)) + 2 * g + r
                    pack_ref[half, piece, 32 * s : 32 * s + 32, :] = got[
                        32 * r : 32 * r + 32, 128 * g : 128 * g + 128]
                    if s == 0:
                        pack_ref[half, piece, 128:ROWS, :] = drops[:, 128 * g : 128 * g + 128]
        return carry

    lax.fori_loop(0, W, states, 0)


def inner_setup(c_ref, bcf_ref, bcr_ref, sc, c3, dsc):
    bcf = bcf_ref[...]
    bcr = bcr_ref[...]
    row = iota((T, T), 0)
    col = iota((T, T), 1)
    sf = mat3_nt(bcf[:, N:], bcf[:, :N])
    sr = mat3_nt(bcr[:, N:], bcr[:, :N])
    sc[...] = jnp.where(row > col, sf, jnp.where(row < col, sr, 0.0))
    c3[...] = jnp.concatenate(split3(c_ref[...]), axis=1)
    dsc[...] = jnp.zeros((T, T), F32)


def inner_pair(i, x_ref, dy_ref, at_ref, sc, c3, y_ref, dx_ref, dsc, rs_ref, cs_ref, xi_ref):
    cols = pl.ds(pl.multiple_of(i * 128, 128), 128)
    xp = x_ref[:, cols]
    dp = dy_ref[:, cols]
    dpt = dp.astype(F32).T.astype(BF16)
    seg_rows = iota((128, 128), 0) // N + 2 * i
    seg_cols = iota((128, 128), 1)
    seg = ones_where((seg_cols < 2 * H) & (seg_cols % H == seg_rows))
    xi_ref[...] += mat2(dp.astype(F32) * xp.astype(F32), seg)
    lane = iota((1, 128), 1)
    row = iota((BLOCK, BLOCK), 0)
    col = iota((BLOCK, BLOCK), 1)
    low = row > col
    up = row < col
    lanes = iota((T, 128), 1)
    y = jnp.zeros((T, 128), F32)
    dut = []
    for k in range(2):
        h = 2 * i + k
        mask = ones_where((lane // N) == k)
        xm = xp * mask
        cross = mat_nt(dp * mask, xp)
        rows3 = iota((384, T), 0) % 128
        cols3 = iota((384, T), 1)
        sel = ones_where(rows3 == h + jnp.where(cols3 < 128, 0, H))
        cb = mat(c3[...], sel)
        af = at_ref[pl.ds(h, 1), :]
        ar = at_ref[pl.ds(H + h, 1), :]
        top = slice(0, BLOCK)
        bot = slice(BLOCK, T)

        def args(rows, columns):
            forward = cb[rows, 0:128] + af[:, columns]
            reverse = cb[rows, 128:256] + ar[:, columns]
            return forward, reverse

        e = {}
        for r in (top, bot):
            for q in (top, bot):
                f, b = args(r, q)
                if r is q:
                    arg = jnp.where(low, f, jnp.where(up, b, FAR))
                else:
                    arg = f if r is bot else b
                e[r is bot, q is bot] = jnp.exp(arg)
        kk = {}
        g = {}
        for r in (top, bot):
            for q in (top, bot):
                key = (r is bot, q is bot)
                kk[key] = sc[r, q] * e[key]
                xx = cross[r, q]
                g[key] = xx * kk[key]
                dsc[r, q] += xx * e[key]
        g0f = jnp.where(low, g[False, False], 0.0)
        g0r = g[False, False] - g0f
        g1f = jnp.where(low, g[True, True], 0.0)
        g1r = g[True, True] - g1f
        rf = jnp.concatenate(
            [jnp.sum(g0f, axis=1, keepdims=True),
             jnp.sum(g[True, False] + g1f, axis=1, keepdims=True)], axis=0)
        rr = jnp.concatenate(
            [jnp.sum(g0r + g[False, True], axis=1, keepdims=True),
             jnp.sum(g1r, axis=1, keepdims=True)], axis=0)
        rs_ref[...] = jnp.where(lanes == h, rf, jnp.where(lanes == H + h, rr, rs_ref[...]))
        cs_ref[pl.ds(h, 1), :] = jnp.concatenate(
            [jnp.sum(g0f + g[True, False], axis=0, keepdims=True),
             jnp.sum(g1f, axis=0, keepdims=True)], axis=1)
        cs_ref[pl.ds(H + h, 1), :] = jnp.concatenate(
            [jnp.sum(g0r, axis=0, keepdims=True),
             jnp.sum(g[False, True] + g1r, axis=0, keepdims=True)], axis=1)
        full = jnp.concatenate(
            [jnp.concatenate([kk[False, False], kk[False, True]], axis=1),
             jnp.concatenate([kk[True, False], kk[True, True]], axis=1)], axis=0)
        hi, lo = split2(full)
        y = y + mat(hi, xm) + mat(lo, xm)
        rows = dpt[N * k : N * (k + 1), :]
        dut.append(mat(rows, hi) + mat(rows, lo))
    y_ref[:, cols] = y
    dx_ref[:, cols] = jnp.concatenate(dut, axis=0).T


def middle_kernel(chips, x_ref, dy_ref, nb_ref, prm_ref, c_ref, step_ref, z_ref, at_ref, bcf_ref,
                  bcr_ref, whi_ref, wlo_ref, pack_ref,
                  mixed_ref, dseq_ref, grad_ref,
                  y_in, dx, dsc, rs, cs, xi, sc, c3, rho, kap, omega, acc, accl,
                  other, sums, inbox, outbox, came, give, carried,
                  s_swap, r_swap, s_in, r_in, s_out, r_out, s_hand, r_hand):
    per = PIECES // chips
    dp = lax.axis_index("dp")
    ctx = lax.axis_index("ctx")
    core = ctx % 2
    me = ctx // 2
    partner = (dp, ctx + 1 - 2 * core)

    def chip_device(k):
        return (dp, 2 * k + core)

    def peer(i):
        return lax.rem(me + 1 + i, chips)

    def remote(src, dst, send, recv, device):
        return pltpu.make_async_remote_copy(
            src_ref=src, dst_ref=dst, send_sem=send, recv_sem=recv,
            device_id=device, device_id_type=MESH,
        )

    def loop(count, body):
        def step(i, carry):
            body(i)
            return carry

        lax.fori_loop(0, count, step, 0)

    barrier = pltpu.get_barrier_semaphore()
    pl.semaphore_signal(barrier, inc=1, device_id=partner, device_id_type=MESH)
    loop(chips - 1, lambda i: pl.semaphore_signal(
        barrier, inc=1, device_id=chip_device(peer(i)), device_id_type=MESH))
    pl.semaphore_wait(barrier, chips)

    def block(k):
        return pl.ds(k * per, per)

    def swap(k):
        return remote(pack_ref.at[1 - core, block(k)], other.at[block(k)],
                      s_swap.at[k], r_swap.at[k], partner)

    loop(chips, lambda i: swap(peer(i)).start())
    first = [core == 0, core == 0, core == 1, core == 1]

    def add_up(k, place):
        swap(k).wait_recv()

        def one(u):
            p = k * per + u
            dm = pack_ref[core, p, 128:ROWS, :]
            dt = other[p, 128:ROWS, :]
            for s in range(4):
                rows = slice(32 * s, 32 * s + 32)
                mine = pack_ref[core, p, rows, :]
                theirs = other[p, rows, :]
                place[u, rows, :] = jnp.where(
                    first[s], dt[s : s + 1] * mine + theirs, dm[s : s + 1] * theirs + mine)
            place[u, 128:ROWS, :] = dm * dt

        loop(per, one)

    def to_owner(k):
        return remote(sums.at[k], inbox.at[me], s_in.at[k], r_in.at[me], chip_device(k))

    def send_sum(i):
        k = peer(i)
        add_up(k, sums.at[k])
        to_owner(k).start()

    loop(chips - 1, send_sum)
    add_up(me, inbox.at[me])

    inner_setup(c_ref, bcf_ref, bcr_ref, sc, c3, dsc)
    rs[...] = jnp.zeros((T, 128), F32)
    cs[...] = jnp.zeros((128, T), F32)
    xi[...] = jnp.zeros((T, 128), F32)
    loop(G, lambda i: inner_pair(
        i, x_ref, dy_ref, at_ref, sc, c3, y_in, dx, dsc, rs, cs, xi))
    for ref in (rho, kap, omega, acc, accl):
        ref[...] = jnp.zeros(ref.shape, F32)

    def got_sum(i):
        k = peer(i)
        remote(sums.at[k], inbox.at[k], s_in.at[k], r_in.at[k], chip_device(k)).wait_recv()

    loop(chips - 1, got_sum)

    def scan(u):
        def up(c, run):
            outbox[c, u, 0:64, :] = run
            drop = inbox[c, u, 128:ROWS, :]
            return jnp.concatenate(
                [drop[0:1] * run[0:32], drop[1:2] * run[32:64]], axis=0) + inbox[c, u, 0:64, :]

        def down(i, run):
            c = chips - 1 - i
            outbox[c, u, 64:128, :] = run
            drop = inbox[c, u, 128:ROWS, :]
            return jnp.concatenate(
                [drop[2:3] * run[0:32], drop[3:4] * run[32:64]], axis=0) + inbox[c, u, 64:128, :]

        def both(i, runs):
            return up(i, runs[0]), down(i, runs[1])

        zero = jnp.zeros((64, 128), F32)
        lax.fori_loop(0, chips, both, (zero, zero))

    loop(per, scan)

    def to_chip(k):
        return remote(outbox.at[k], came.at[me], s_out.at[k], r_out.at[me], chip_device(k))

    loop(chips - 1, lambda i: to_chip(peer(i)).start())
    came[me] = outbox[me]

    lane = iota((T, 128), 1)
    c = c_ref[...]
    step = step_ref[...]
    bcf = bcf_ref[...]
    bcr = bcr_ref[...]
    last = jnp.where(lane[0:1] < H, c[T - 1 : T], c[0:1])
    e2 = lanes2(jnp.exp(c))
    tail2 = lanes2(jnp.exp(last - c) * step)
    sig_f = jnp.sum(bcf[:, :N] * bcf[:, N:], axis=1, keepdims=True)
    sig_r = jnp.sum(bcr[:, :N] * bcr[:, N:], axis=1, keepdims=True)
    sigma = jnp.where(lane < H, sig_f, jnp.where(lane < 2 * H, sig_r, 0.0))
    coef3 = jnp.concatenate(split3(sigma * step + prm_ref[2:3, :]), axis=1)

    def left3(a):
        hi, lo = split2(a)
        return jnp.concatenate([hi, lo, hi], axis=1)

    l_bf, l_cf = left3(bcf[:, :N]), left3(bcf[:, N:])
    l_br, l_cr = left3(bcr[:, :N]), left3(bcr[:, N:])

    def group_of(i):
        return lax.rem(me * per // 2 + i, 8)

    def hand(g):
        spot = pl.ds(2 * g, 2)
        return remote(give.at[spot], carried.at[core, spot], s_hand.at[g], r_hand.at[g], partner)

    def receive(i):
        g = group_of(i)
        for r in range(2):
            p = 2 * g + r
            k = p // per

            if per == 1 or r == 0:
                @pl.when((k != me) & (p % per == 0))
                def _():
                    remote(outbox.at[k], came.at[k], s_out.at[k], r_out.at[k],
                           chip_device(k)).wait_recv()

            dm = pack_ref[core, p, 128:ROWS, :]
            dt = other[p, 128:ROWS, :]
            for s in range(4):
                rows = slice(32 * s, 32 * s + 32)
                got = came[k, p % per, rows, :]
                mine = pack_ref[core, p, rows, :]
                theirs = other[p, rows, :]
                carried[core, p, rows, :] = jnp.where(first[s], got, dt[s : s + 1] * got + theirs)
                give[p, rows, :] = jnp.where(first[s], dm[s : s + 1] * got + mine, got)
        hand(g).start()

    def work(i):
        g = group_of(i)
        remote(give.at[pl.ds(2 * g, 2)], carried.at[1 - core, pl.ds(2 * g, 2)],
               s_hand.at[g], r_hand.at[g], partner).wait_recv()
        groups = (8 * core + g, 8 * (1 - core) + g)
        places = [pl.ds(pl.multiple_of(j * 128, 128), 128) for j in groups]

        def wide(ref):
            return jnp.concatenate([ref[:, p] for p in places], axis=1)

        def state(s):
            rows = slice(32 * s, 32 * s + 32)
            return jnp.concatenate(
                [jnp.concatenate([carried[h, 2 * g, rows, :], carried[h, 2 * g + 1, rows, :]], axis=0)
                 for h in (core, 1 - core)], axis=1)

        state_f, adj_r, state_r, adj_f = state(0), state(1), state(2), state(3)
        sel_f, sel_r = spread(*groups)
        two_f, two_r = twice(sel_f), twice(sel_r)
        ef, er = mat(e2, two_f), mat(e2, two_r)
        tf, tr = mat(tail2, two_f), mat(tail2, two_r)
        one = sel_f + sel_r
        coef = mat(coef3, jnp.concatenate([one, one, one], axis=0))
        xj = wide(x_ref).astype(F32)
        dj = wide(dy_ref).astype(F32)
        wf, wr = tf * xj, tr * xj
        cuts = [split2(a) for a in (state_f, state_r, adj_f, adj_r)]

        def times(left, cut):
            return mat(left, jnp.concatenate([cut[0], cut[0], cut[1]], axis=0))

        yf = ef * times(l_cf, cuts[0])
        yr = er * times(l_cr, cuts[1])
        vf = times(l_bf, cuts[2])
        vr = times(l_br, cuts[3])
        out = wide(y_in) + (yf + yr) + coef * xj
        more = wide(dx) + (tf * vf + tr * vr) + coef * dj
        for n, p in enumerate(places):
            mixed_ref[:, p] = out[:, 128 * n : 128 * n + 128].astype(BF16)
            dx[:, p] = more[:, 128 * n : 128 * n + 128]
        back_f = sel_f.astype(F32).T.astype(BF16)
        back_r = sel_r.astype(F32).T.astype(BF16)
        rho[...] += mat2(dj * yf, back_f) + mat2(dj * yr, back_r)
        kap[...] += mat2(wf * vf, back_f) + mat2(wr * vr, back_r)
        in_f = jnp.sum(state_f * adj_f, axis=0, keepdims=True)
        in_r = jnp.sum(state_r * adj_r, axis=0, keepdims=True)
        omega[...] += (exact_right(jnp.broadcast_to(in_f, (8, 256)), back_f)
                       + exact_right(jnp.broadcast_to(in_r, (8, 256)), back_r))
        for n, (left, cut) in enumerate(zip((ef * dj, er * dj, wf, wr), cuts)):
            hi, lo = split2(left)
            acc[n] += mat_nt(hi, jnp.concatenate(cut, axis=0))
            accl[n] += mat_nt(lo, cut[0])

    def arrive(i):
        @pl.when(i < 8)
        def _():
            receive(i)

        @pl.when(i > 0)
        def _():
            work(i - 1)

    loop(9, arrive)

    def total(n):
        a = acc[n]
        return a[:, :N] + a[:, N:] + accl[n]

    z = z_ref[...]
    row = iota((T, T), 0)
    col = iota((T, T), 1)
    colsum = cs[...].T
    kappa = kap[...]
    through = rs[...] - colsum + rho[...]
    d_fall = jnp.where(
        lane < H,
        exact_left(ones_where(row <= col), through) + exact_left(ones_where(row > col), kappa),
        exact_left(ones_where(row >= col), through) + exact_left(ones_where(row < col), kappa),
    ) + omega[0:1, :] * jnp.exp(last)
    small = jnp.exp(-jnp.abs(z))
    soft = jnp.maximum(z, 0.0) + jnp.log1p(small)
    sigmoid = jnp.where(z >= 0.0, 1.0, small) / (1.0 + small)
    ratio = jnp.where(z < -30.0, 1.0, sigmoid / jnp.maximum(soft, 1e-30))
    ksi = xi[...]
    diag = step * ksi
    straight = colsum + kappa + sigma * diag
    dz = straight * ratio - prm_ref[1:2, :] * d_fall * sigmoid * keep_column(nb_ref)
    dz = jnp.where(lane < 2 * H, dz, 0.0)

    ds_f = jnp.sum(jnp.where(lane < H, diag, 0.0), axis=1, keepdims=True)
    ds_r = jnp.sum(jnp.where((lane >= H) & (lane < 2 * H), diag, 0.0), axis=1, keepdims=True)
    mixing = dsc[...]
    turned = mixing.T
    eq = row == col
    m_f = jnp.where(eq, ds_f, jnp.where(row > col, mixing, 0.0))
    m_r = jnp.where(eq, ds_r, jnp.where(row < col, mixing, 0.0))
    mt_f = jnp.where(eq, ds_f, jnp.where(row < col, turned, 0.0))
    mt_r = jnp.where(eq, ds_r, jnp.where(row > col, turned, 0.0))
    d_bcf = jnp.concatenate([total(2) + mat3(mt_f, bcf[:, N:]), total(0) + mat3(m_f, bcf[:, :N])], axis=1)
    d_bcr = jnp.concatenate([total(3) + mat3(mt_r, bcr[:, N:]), total(1) + mat3(m_r, bcr[:, :N])], axis=1)
    dproj = jnp.concatenate([dz, d_bcf, d_bcr], axis=1)
    p_hi, p_lo = split2(dproj)
    p_cat = jnp.concatenate([p_hi, p_lo, p_hi], axis=1)

    r128 = iota((128, 128), 0)
    c128 = iota((128, 128), 1)
    fold = ones_where(((r128 < H) & (r128 == c128))
                      | ((r128 >= H) & (r128 < 2 * H) & (r128 + c128 == 2 * H - 1)))
    vectors = jnp.concatenate(
        [jnp.sum(dz, axis=0, keepdims=True),
         -jnp.sum(step * d_fall, axis=0, keepdims=True),
         jnp.sum(ksi, axis=0, keepdims=True),
         jnp.zeros((5, 128), F32)], axis=0)
    tiles_all = grad_ref.shape[0]
    grad_ref[20 * G : tiles_all] = jnp.zeros((tiles_all - 20 * G, 8, 128), F32)
    grad_ref[20 * G] = exact_right(vectors, fold)

    dz_t = dz.T
    f_t = jnp.concatenate([dz_t[0:H], d_bcf.T], axis=0)
    r_hi, r_lo = split2(jnp.concatenate([dz_t[H : 2 * H], d_bcr.T], axis=0))
    f_hi, f_lo = split2(f_t)
    rev = backwards(H)

    def ordered(a):
        return jnp.concatenate([mat(rev, a[0:H]).astype(BF16), a[H:]], axis=0)

    left = jnp.concatenate(
        [jnp.concatenate([f_hi, ordered(r_hi)], axis=1),
         jnp.concatenate([f_lo, ordered(r_lo)], axis=1)], axis=0)
    flip = backwards(256)

    def final(i):
        cols = pl.ds(pl.multiple_of(i * 256, 256), 256)
        far = pl.ds(pl.multiple_of((W - 1 - i) * 256, 256), 256)
        w_hi = whi_ref[:, cols]
        w_cat = jnp.concatenate([w_hi, w_hi, wlo_ref[:, cols]], axis=0)
        dseq_ref[:, cols] = (dx[:, cols] + mat(p_cat, w_cat)).astype(BF16)
        right = jnp.concatenate(
            [x_ref[:, cols], mat(x_ref[:, far], flip).astype(BF16)], axis=0)
        grads = mat(left, right)
        grads = grads[0:160] + grads[160:320]
        for r in range(20):
            for n in range(2):
                grad_ref[r * G + 2 * i + n] = grads[8 * r : 8 * r + 8, 128 * n : 128 * n + 128]

    loop(W, final)

    loop(chips, lambda k: swap(k).wait_send())
    loop(chips - 1, lambda i: to_owner(peer(i)).wait_send())
    loop(chips - 1, lambda i: to_chip(peer(i)).wait_send())
    loop(8, lambda g: hand(g).wait_send())


def sum_kernel(halves, depth, g_ref, dt_ref, b_ref, c_ref, vec_ref, out_ref, from_core, held, from_plane, part, from_z, full,
               s_core, r_core, s_plane, r_plane, s_z, r_z, s_zg, r_zg, s_pg, r_pg, s_cg, r_cg):
    dp = lax.axis_index("dp")
    ctx = lax.axis_index("ctx")
    plane = g_ref.shape[0] // 2
    tiles = g_ref.shape[1]
    zt = from_z.shape[1]
    core = ctx % 2
    z = (ctx // 2) % depth
    me = dp * halves + ctx // (2 * depth)
    partner = (dp, ctx + 1 - 2 * core)

    def plane_device(k):
        return (k // halves, ((k % halves) * depth + z) * 2 + core)

    def z_device(j):
        return (dp, ((ctx // (2 * depth)) * depth + j) * 2 + core)

    def peer(i):
        return lax.rem(me + 1 + i, plane)

    def z_peer(i):
        return lax.rem(z + 1 + i, depth)

    def remote(src, dst, send, recv, device):
        return pltpu.make_async_remote_copy(
            src_ref=src, dst_ref=dst, send_sem=send, recv_sem=recv,
            device_id=device, device_id_type=MESH,
        )

    def loop(count, body):
        def step(i, carry):
            body(i)
            return carry

        lax.fori_loop(0, count, step, 0)

    barrier = pltpu.get_barrier_semaphore()
    pl.semaphore_signal(barrier, inc=1, device_id=partner, device_id_type=MESH)
    loop(plane - 1, lambda i: pl.semaphore_signal(
        barrier, inc=1, device_id=plane_device(peer(i)), device_id_type=MESH))
    loop(depth - 1, lambda i: pl.semaphore_signal(
        barrier, inc=1, device_id=z_device(z_peer(i)), device_id_type=MESH))
    pl.semaphore_wait(barrier, plane + depth - 1)

    def core_copy(k):
        return remote(g_ref.at[(1 - core) * plane + k], from_core.at[k],
                      s_core.at[k], r_core.at[k], partner)

    def plane_copy(k):
        return remote(held.at[k], from_plane.at[me], s_plane.at[k], r_plane.at[me],
                      plane_device(k))

    loop(plane, lambda i: core_copy(peer(i)).start())

    def add_core(i):
        k = peer(i)
        core_copy(k).wait_recv()
        held[k] = g_ref[core * plane + k] + from_core[k]

    def forward(i):
        add_core(i)
        plane_copy(peer(i)).start()

    loop(plane - 1, forward)
    add_core(plane - 1)
    part[...] = jnp.zeros(part.shape, F32)
    part[0:tiles] = held[me]

    def add_plane(i):
        k = lax.rem(me + plane - 1 - i, plane)
        remote(held.at[k], from_plane.at[k], s_plane.at[k], r_plane.at[k],
               plane_device(k)).wait_recv()
        part[0:tiles] += from_plane[k]

    loop(plane - 1, add_plane)

    def z_copy(j):
        return remote(part.at[pl.ds(j * zt, zt)], from_z.at[z], s_z.at[j], r_z.at[z], z_device(j))

    loop(depth - 1, lambda i: z_copy(z_peer(i)).start())
    full[pl.ds(z * zt, zt)] = part[pl.ds(z * zt, zt)]

    def add_z(i):
        j = z_peer(i)
        remote(part.at[pl.ds(j * zt, zt)], from_z.at[j], s_z.at[j], r_z.at[j],
               z_device(j)).wait_recv()
        full[pl.ds(z * zt, zt)] += from_z[j]

    loop(depth - 1, add_z)

    def z_share(j):
        return remote(full.at[pl.ds(z * zt, zt)], full.at[pl.ds(z * zt, zt)],
                      s_zg.at[j], r_zg.at[z], z_device(j))

    loop(depth - 1, lambda i: z_share(z_peer(i)).start())

    def z_got(i):
        j = z_peer(i)
        remote(full.at[pl.ds(j * zt, zt)], full.at[pl.ds(j * zt, zt)],
               s_zg.at[j], r_zg.at[j], z_device(j)).wait_recv()

    loop(depth - 1, z_got)
    mine = core * plane + me
    out_ref[mine] = full[0:tiles]

    def plane_share(k):
        return remote(out_ref.at[mine], out_ref.at[mine], s_pg.at[k], r_pg.at[me], plane_device(k))

    def core_share(k):
        return remote(out_ref.at[core * plane + k], out_ref.at[core * plane + k],
                      s_cg.at[k], r_cg.at[k], partner)

    loop(plane - 1, lambda i: plane_share(peer(i)).start())
    core_share(me).start()

    def plane_got(i):
        k = lax.rem(me + plane - 1 - i, plane)
        spot = out_ref.at[core * plane + k]
        remote(spot, spot, s_pg.at[k], r_pg.at[k], plane_device(k)).wait_recv()
        core_share(k).start()

    loop(plane - 1, plane_got)

    def core_got(k):
        spot = out_ref.at[(1 - core) * plane + k]
        remote(spot, spot, s_cg.at[k], r_cg.at[k], partner).wait_recv()

    loop(plane, core_got)

    def unpack(j):
        cols = pl.ds(pl.multiple_of(j * 128, 128), 128)
        for r in range(20):
            ref, base = (dt_ref, 0) if r < 4 else (b_ref, 4) if r < 12 else (c_ref, 12)
            n = r * G + j
            ref[8 * (r - base) : 8 * (r - base) + 8, cols] = out_ref[n // tiles, n % tiles]

    loop(G, unpack)
    vec_ref[...] = out_ref[20 * G // tiles, 20 * G % tiles]
    loop(plane, lambda k: core_copy(k).wait_send())
    loop(plane, lambda k: core_share(k).wait_send())
    loop(plane - 1, lambda i: plane_copy(peer(i)).wait_send())
    loop(plane - 1, lambda i: plane_share(peer(i)).wait_send())
    loop(depth - 1, lambda i: z_copy(z_peer(i)).wait_send())
    loop(depth - 1, lambda i: z_share(z_peer(i)).wait_send())


def sds(shape, dtype=F32):
    return jax.ShapeDtypeStruct(shape, dtype)


def on_device(sizes, sequence, n_blocks, w_dt, dt_bias, decay_rate, w_b, w_c, d_skip, cotangent):
    dps, ctxs = sizes
    chips = ctxs // 2
    halves = 2 if ctxs % 4 == 0 else 1
    depth = chips // halves
    plane = dps * halves
    tiles = -(-(20 * G + 1) // (2 * plane))
    zt = -(-tiles // depth)
    per = PIECES // chips
    x = sequence[0]
    dy = cotangent[0]
    dma = pltpu.SemaphoreType.DMA
    vmem = pltpu.VMEM

    outs = [sds((2, PIECES, ROWS, 128)), sds((8, 128)), sds((T, 128)), sds((T, 128)), sds((T, 128)),
            sds((128, T)), sds((T, 128)), sds((T, 128)), sds((384, D), BF16), sds((384, D), BF16)]
    pack, prm, c, step, z, at, bcf, bcr, whi, wlo = pl.pallas_call(
        front_kernel,
        out_shape=outs,
        in_specs=[VMEM, VMEM, SMEM] + [VMEM] * 6,
        out_specs=[VMEM] * len(outs),
        compiler_params=pltpu.CompilerParams(vmem_limit_bytes=ALL),
    )(x, dy, n_blocks, w_dt.T, w_b.T, w_c.T, dt_bias[None], decay_rate[None], d_skip[None])

    block = (chips, per)
    mixed, dseq, grads = pl.pallas_call(
        functools.partial(middle_kernel, chips),
        out_shape=[sds((T, D), BF16), sds((T, D), BF16), sds((2 * plane * tiles, 8, 128))],
        in_specs=[VMEM, VMEM, SMEM] + [VMEM] * 10,
        out_specs=[VMEM] * 3,
        scratch_shapes=[
            vmem((T, D), F32), vmem((T, D), F32), vmem((T, T), F32), vmem((T, 128), F32),
            vmem((128, T), F32), vmem((T, 128), F32), vmem((T, T), F32), vmem((T, 384), BF16),
            vmem((T, 128), F32), vmem((T, 128), F32), vmem((8, 128), F32),
            vmem((4, T, 128), F32), vmem((4, T, N), F32),
            vmem((PIECES, ROWS, 128), F32), vmem(block + (ROWS, 128), F32),
            vmem(block + (ROWS, 128), F32), vmem(block + (128, 128), F32),
            vmem(block + (128, 128), F32), vmem((PIECES, 128, 128), F32),
            vmem((2, PIECES, 128, 128), F32),
        ] + [dma((chips,))] * 6 + [dma((8,))] * 2,
        compiler_params=pltpu.CompilerParams(
            vmem_limit_bytes=ALL, collective_id=0, has_side_effects=True),
    )(x, dy, n_blocks, prm, c, step, z, at, bcf, bcr, whi, wlo, pack)

    grad_dt, grad_b, grad_c, vectors = pl.pallas_call(
        functools.partial(sum_kernel, halves, depth),
        out_shape=[sds((H, D)), sds((N, D)), sds((N, D)), sds((8, 128))],
        in_specs=[VMEM],
        out_specs=[VMEM] * 4,
        scratch_shapes=[
            vmem((2 * plane, tiles, 8, 128), F32),
            vmem((plane, tiles, 8, 128), F32),
            vmem((plane, tiles, 8, 128), F32),
            vmem((plane, tiles, 8, 128), F32),
            vmem((depth * zt, 8, 128), F32),
            vmem((depth, zt, 8, 128), F32),
            vmem((depth * zt, 8, 128), F32),
        ] + [dma((plane,))] * 4 + [dma((depth,))] * 4 + [dma((plane,))] * 4,
        compiler_params=pltpu.CompilerParams(
            vmem_limit_bytes=LIMIT, collective_id=1, has_side_effects=True),
    )(grads.reshape(2 * plane, tiles, 8, 128))

    return (mixed[None], dseq[None], grad_dt.T, vectors[0, :H], vectors[1, :H],
            grad_b.T, grad_c.T, vectors[2, :H])


def solution(mesh):
    sizes = (mesh.shape["dp"], mesh.shape["ctx"])
    return jax.shard_map(
        functools.partial(on_device, sizes),
        mesh=mesh,
        in_specs=(
            P("dp", "ctx", None),
            P("dp", "ctx"),
            P(), P(), P(), P(), P(), P(),
            P("dp", "ctx", None),
        ),
        out_specs=(P("dp", "ctx", None), P("dp", "ctx", None), P(), P(), P(), P(), P(), P()),
        check_vma=False,
    )
```

```python
import functools

import jax
import jax.numpy as jnp
from jax import lax
from jax.experimental import pallas as pl
from jax.experimental.pallas import tpu as pltpu
from jax.sharding import PartitionSpec as P

F32 = jnp.float32
BF16 = jnp.bfloat16
BLOCK = 128
T = 256
D = 2048
H = 32
N = 64
G = 16
W = D // 256
MESH = pl.DeviceIdType.MESH
VMEM = pl.BlockSpec(memory_space=pltpu.VMEM)
SMEM = pl.BlockSpec(memory_space=pltpu.SMEM)
ALL = 62 * 1024 * 1024
PIECES = 16
ROWS = (72, 64)
TILES = 20
FAR = -1e30
EARLY = 12


def iota(shape, axis):
    return lax.broadcasted_iota(jnp.int32, shape, axis)


def mat(a, b):
    return lax.dot_general(a, b, (((1,), (0,)), ((), ())), preferred_element_type=F32)


def mat_nt(a, b):
    return lax.dot_general(a, b, (((1,), (1,)), ((), ())), preferred_element_type=F32)


def split2(a):
    hi = a.astype(BF16)
    return hi, (a - hi.astype(F32)).astype(BF16)


def split3(a):
    hi = a.astype(BF16)
    rest = a - hi.astype(F32)
    mid = rest.astype(BF16)
    return hi, mid, (rest - mid.astype(F32)).astype(BF16)


def mat2(a, exact):
    hi, lo = split2(a)
    return mat(hi, exact) + mat(lo, exact)


def mat3(a, b):
    ah, al = split2(a)
    bh, bl = split2(b)
    return mat(ah, bh) + (mat(al, bh) + mat(ah, bl))


def mat3_nt(a, b):
    ah, al = split2(a)
    bh, bl = split2(b)
    return mat_nt(ah, bh) + (mat_nt(al, bh) + mat_nt(ah, bl))


def exact_left(zero_one, a):
    hi, mid, lo = split3(a)
    return mat(zero_one, hi) + (mat(zero_one, mid) + mat(zero_one, lo))


def exact_right(a, zero_one):
    hi, mid, lo = split3(a)
    return mat(hi, zero_one) + (mat(mid, zero_one) + mat(lo, zero_one))


def ones_where(condition):
    return jnp.where(condition, 1.0, 0.0).astype(BF16)


def backwards(size):
    return ones_where(iota((size, size), 0) + iota((size, size), 1) == size - 1)


def keep_column(nb_ref):
    first = 1.0 - nb_ref[0, 0].astype(F32)
    second = 1.0 - nb_ref[0, 1].astype(F32)
    return jnp.where(iota((T, 1), 0) < BLOCK, first, second)


def spread(first, second):
    rows = iota((128, 256), 0)
    cols = iota((128, 256), 1)
    head = jnp.where(cols < 128, 2 * first, 2 * second) + (cols % 128) // N
    return ones_where(rows == head), ones_where(rows == head + H)


def twice(a):
    return jnp.concatenate([a, a], axis=0)


def lanes2(a):
    return jnp.concatenate(split2(a), axis=1)


def inner_setup(c, bcf, bcr, sc, c3, dsc):
    row = iota((T, T), 0)
    col = iota((T, T), 1)
    sf = mat3_nt(bcf[:, N:], bcf[:, :N])
    sr = mat3_nt(bcr[:, N:], bcr[:, :N])
    sc[...] = jnp.where(row > col, sf, jnp.where(row < col, sr, 0.0))
    c3[...] = jnp.concatenate(split3(c), axis=1)
    dsc[...] = jnp.zeros((T, T), F32)


def inner_pair(i, x_ref, dy_ref, at_ref, sc, c3, y_ref, dx_ref, dsc, rs_ref, cs_ref, xi_ref):
    cols = pl.ds(pl.multiple_of(i * 128, 128), 128)
    xp = x_ref[:, cols]
    dp = dy_ref[:, cols]
    dpt = dp.astype(F32).T.astype(BF16)
    seg_rows = iota((128, 128), 0) // N + 2 * i
    seg_cols = iota((128, 128), 1)
    seg = ones_where((seg_cols < 2 * H) & (seg_cols % H == seg_rows))
    xi_ref[...] += mat2(dp.astype(F32) * xp.astype(F32), seg)
    lane = iota((1, 128), 1)
    row = iota((BLOCK, BLOCK), 0)
    col = iota((BLOCK, BLOCK), 1)
    low = row > col
    up = row < col
    lanes = iota((T, 128), 1)
    y = jnp.zeros((T, 128), F32)
    dut = []
    for k in range(2):
        h = 2 * i + k
        mask = ones_where((lane // N) == k)
        xm = xp * mask
        cross = mat_nt(dp * mask, xp)
        rows3 = iota((384, T), 0) % 128
        cols3 = iota((384, T), 1)
        sel = ones_where(rows3 == h + jnp.where(cols3 < 128, 0, H))
        cb = mat(c3[...], sel)
        af = at_ref[pl.ds(h, 1), :]
        ar = at_ref[pl.ds(H + h, 1), :]
        top = slice(0, BLOCK)
        bot = slice(BLOCK, T)

        def args(rows, columns):
            forward = cb[rows, 0:128] + af[:, columns]
            reverse = cb[rows, 128:256] + ar[:, columns]
            return forward, reverse

        e = {}
        for r in (top, bot):
            for q in (top, bot):
                f, b = args(r, q)
                if r is q:
                    arg = jnp.where(low, f, jnp.where(up, b, FAR))
                else:
                    arg = f if r is bot else b
                e[r is bot, q is bot] = jnp.exp(arg)
        kk = {}
        g = {}
        for r in (top, bot):
            for q in (top, bot):
                key = (r is bot, q is bot)
                kk[key] = sc[r, q] * e[key]
                xx = cross[r, q]
                g[key] = xx * kk[key]
                dsc[r, q] += xx * e[key]
        g0f = jnp.where(low, g[False, False], 0.0)
        g0r = g[False, False] - g0f
        g1f = jnp.where(low, g[True, True], 0.0)
        g1r = g[True, True] - g1f
        rf = jnp.concatenate(
            [jnp.sum(g0f, axis=1, keepdims=True),
             jnp.sum(g[True, False] + g1f, axis=1, keepdims=True)], axis=0)
        rr = jnp.concatenate(
            [jnp.sum(g0r + g[False, True], axis=1, keepdims=True),
             jnp.sum(g1r, axis=1, keepdims=True)], axis=0)
        rs_ref[...] = jnp.where(lanes == h, rf, jnp.where(lanes == H + h, rr, rs_ref[...]))
        cs_ref[pl.ds(h, 1), :] = jnp.concatenate(
            [jnp.sum(g0f + g[True, False], axis=0, keepdims=True),
             jnp.sum(g1f, axis=0, keepdims=True)], axis=1)
        cs_ref[pl.ds(H + h, 1), :] = jnp.concatenate(
            [jnp.sum(g0r, axis=0, keepdims=True),
             jnp.sum(g[False, True] + g1r, axis=0, keepdims=True)], axis=1)
        full = jnp.concatenate(
            [jnp.concatenate([kk[False, False], kk[False, True]], axis=1),
             jnp.concatenate([kk[True, False], kk[True, True]], axis=1)], axis=0)
        hi, lo = split2(full)
        y = y + mat(hi, xm) + mat(lo, xm)
        rows = dpt[N * k : N * (k + 1), :]
        dut.append(mat(rows, hi) + mat(rows, lo))
    y_ref[:, cols] = y
    dx_ref[:, cols] = jnp.concatenate(dut, axis=0).T


def kernel(chips, halves, depth, x_ref, dy_ref, nb_ref, wdt_ref, wb_ref, wc_ref,
           bias_ref, rate_ref, skip_ref,
           mixed_ref, dseq_ref, dt_ref, b_ref, c_ref, vec_ref,
           whi, wlo, at_ref, y_in, dx, dsc, rs, cs, xi, sc, c3, rho, kap, omega, acc, accl,
           pack_up, pack_down, other_up, other_down, sums_up, sums_down, in_up, in_down,
           out_up, out_down, came_up, came_down, give, carried,
           grad, all_ref, from_core, held, from_plane, part, from_z, full,
           s_swap, r_swap, s_in, r_in, s_out, r_out, s_hand, r_hand,
           s_core, r_core, s_plane, r_plane, s_z, r_z, s_zg, r_zg, s_pg, r_pg, s_cg, r_cg):
    per = PIECES // chips
    pack, other = (pack_up, pack_down), (other_up, other_down)
    sums, inbox = (sums_up, sums_down), (in_up, in_down)
    outbox, came = (out_up, out_down), (came_up, came_down)
    plane = held.shape[0]
    tiles = held.shape[1]
    zt = from_z.shape[1]
    dp = lax.axis_index("dp")
    ctx = lax.axis_index("ctx")
    core = ctx % 2
    chip = ctx // 2
    z_me = chip % depth
    p_me = dp * halves + chip // depth
    partner = (dp, ctx + 1 - 2 * core)

    def chip_device(k):
        return (dp, 2 * k + core)

    def chip_peer(i):
        return lax.rem(chip + 1 + i, chips)

    def plane_device(k):
        return (k // halves, ((k % halves) * depth + z_me) * 2 + core)

    def plane_peer(i):
        return lax.rem(p_me + 1 + i, plane)

    def z_device(k):
        return (dp, ((chip // depth) * depth + k) * 2 + core)

    def z_peer(i):
        return lax.rem(z_me + 1 + i, depth)

    def remote(src, dst, send, recv, device):
        return pltpu.make_async_remote_copy(
            src_ref=src, dst_ref=dst, send_sem=send, recv_sem=recv,
            device_id=device, device_id_type=MESH,
        )

    def loop(count, body, start=0):
        def step(i, carry):
            body(i)
            return carry

        lax.fori_loop(start, count, step, 0)

    barrier = pltpu.get_barrier_semaphore()
    pl.semaphore_signal(barrier, inc=1, device_id=partner, device_id_type=MESH)
    loop(chips - 1, lambda i: pl.semaphore_signal(
        barrier, inc=1, device_id=chip_device(chip_peer(i)), device_id_type=MESH))
    loop(plane - 1, lambda i: pl.semaphore_signal(
        barrier, inc=1, device_id=plane_device(plane_peer(i)), device_id_type=MESH))

    flip = backwards(256)
    rev = backwards(H)
    both = ones_where((iota((H, 128), 1) == iota((H, 128), 0))
                      | (iota((H, 128), 1) + iota((H, 128), 0) == 2 * H - 1))
    bias, rate, skip = (
        exact_right(jnp.broadcast_to(ref[...], (8, H)), both)[0:1]
        for ref in (bias_ref, rate_ref, skip_ref)
    )

    def cut(i, carry):
        here = pl.ds(pl.multiple_of(i * 256, 256), 256)
        there = pl.ds(pl.multiple_of((W - 1 - i) * 256, 256), 256)
        raw = jnp.concatenate([wdt_ref[:, here], wb_ref[:, here], wc_ref[:, here]], axis=0)
        hi, lo = split2(raw)
        turned = mat(jnp.concatenate([hi, lo], axis=0), flip).astype(BF16)
        for ref, own, far in ((whi, hi, turned[0:160]), (wlo, lo, turned[160:320])):
            ref[0:H, here] = own[0:H]
            ref[128:256, here] = own[H:160]
            ref[H : 2 * H, there] = mat(rev, far[0:H]).astype(BF16)
            ref[256:384, there] = far[H:160]
            ref[2 * H : 128, here] = jnp.zeros((2 * H, 256), BF16)
        return carry

    lax.fori_loop(0, W, cut, 0, unroll=2)

    x = x_ref[...]
    proj = mat_nt(x, whi[...]) + mat_nt(x, wlo[...])
    lane = iota((T, 128), 1)
    row = iota((T, T), 0)
    col = iota((T, T), 1)
    keep = keep_column(nb_ref)
    z = proj[:, 0:128] + bias
    soft = jnp.maximum(z, 0.0) + jnp.log1p(jnp.exp(-jnp.abs(z)))
    step = jnp.where(lane < 2 * H, soft * keep, 0.0)
    fall = -step * rate
    c = jnp.where(
        lane < H,
        exact_left(ones_where(row >= col), fall),
        exact_left(ones_where(row <= col), fall),
    )
    last = jnp.where(lane[0:1] < H, c[T - 1 : T], c[0:1])
    at_ref[...] = jnp.where(step > 0.0, jnp.log(jnp.maximum(step, 1e-37)) - c, FAR).T
    bcf = proj[:, 128:256]
    bcr = proj[:, 256:384]
    e2 = lanes2(jnp.exp(c))
    tail2 = lanes2(jnp.exp(last - c) * step)
    decay8 = jnp.broadcast_to(jnp.exp(last), (8, 128))
    tf_hi, tf_lo = split2(bcf.T)
    tr_hi, tr_lo = split2(bcr.T)

    lefts = [
        jnp.concatenate([hi[span], lo[span]], axis=0)
        for hi, lo, span in (
            (tf_hi, tf_lo, slice(0, N)),
            (tr_hi, tr_lo, slice(N, 2 * N)),
            (tr_hi, tr_lo, slice(0, N)),
            (tf_hi, tf_lo, slice(N, 2 * N)),
        )
    ]
    first = (core == 0, core == 1)

    def block(i):
        return lax.rem(i + chip * per // 4, 4)

    def swap(r, q):
        spot = pl.ds(4 * q, 4)
        return remote(pack[r].at[1 - core, spot], other[r].at[spot],
                      s_swap.at[r, q], r_swap.at[r, q], partner)

    def to_owner(r, p):
        return remote(sums[r].at[p, pl.ds(0, ROWS[r])], in_piece(r, chip, p % per),
                      s_in.at[r, p], r_in.at[r, chip * per + p % per], chip_device(p // per))

    def in_piece(r, k, u):
        return inbox[r].at[k, u]

    def local_states(r, half, q):
        i = 4 * half + q
        cols = pl.ds(pl.multiple_of(i * 256, 256), 256)
        sel_f, sel_r = spread(2 * i, 2 * i + 1)
        two_f, two_r = twice(sel_f), twice(sel_r)
        xj = x_ref[:, cols].astype(F32)
        dj = dy_ref[:, cols].astype(F32)
        if r == 0:
            rights = mat(tail2, two_f) * xj, mat(e2, two_r) * dj
            drops = jnp.where(iota((8, 256), 0) == 0,
                              exact_right(decay8, sel_f), exact_right(decay8, sel_r))
        else:
            rights = mat(tail2, two_r) * xj, mat(e2, two_f) * dj
        for s in range(2):
            left = lefts[2 * r + s]
            hi, lo = split2(rights[s])
            wide = mat(left, hi)
            got = wide[0:N] + wide[N : 2 * N] + mat(left[0:N], lo)
            for g in range(2):
                lanes = slice(128 * g, 128 * g + 128)
                for h in range(2):
                    p = 4 * q + 2 * g + h
                    pack[r][half, p, 32 * s : 32 * s + 32, :] = got[32 * h : 32 * h + 32, lanes]
                    if r == 0 and s == 0:
                        pack[r][half, p, 64:72, :] = drops[:, lanes]

    def drop_rows(r, p):
        mine = pack_up[core, p, 64:72, :]
        theirs = other_up[p, 64:72, :]
        order = (0, 1) if r == 0 else (1, 0)
        return [(mine[n : n + 1], theirs[n : n + 1]) for n in order]

    def add_up(r, q):
        swap(r, q).wait_recv()
        for n in range(4):
            p = 4 * q + n
            own = p // per == chip
            drops = drop_rows(r, p)
            out = []
            for s in range(2):
                rows = slice(32 * s, 32 * s + 32)
                dm, dt = drops[s]
                mine = pack[r][core, p, rows, :]
                theirs = other[r][p, rows, :]
                out.append(jnp.where(first[r], dt * mine + theirs, dm * theirs + mine))
            if r == 0:
                out.append(pack_up[core, p, 64:72, :] * other_up[p, 64:72, :])
            whole = jnp.concatenate(out, axis=0)

            @pl.when(own)
            def _():
                inbox[r][chip, p % per] = whole

            @pl.when(jnp.logical_not(own))
            def _():
                sums[r][p] = whole
                to_owner(r, p).start()

    pl.semaphore_wait(barrier, plane + chips - 1)
    for r in range(2):
        def states(i, r=r):
            @pl.when(i < 4)
            def _():
                q = block(i)
                local_states(r, 1 - core, q)
                swap(r, q).start()
                local_states(r, core, q)

            @pl.when(i > 0)
            def _():
                add_up(r, block(i - 1))

        loop(5, states)

    inner_setup(c, bcf, bcr, sc, c3, dsc)
    rs[...] = jnp.zeros((T, 128), F32)
    cs[...] = jnp.zeros((128, T), F32)
    xi[...] = jnp.zeros((T, 128), F32)
    for ref in (rho, kap, omega, acc, accl):
        ref[...] = jnp.zeros(ref.shape, F32)

    def inner(i):
        inner_pair(i, x_ref, dy_ref, at_ref, sc, c3, y_in, dx, dsc, rs, cs, xi)

    def to_chip(r, k):
        return remote(outbox[r].at[k], came[r].at[chip],
                      s_out.at[r, k], r_out.at[r, chip], chip_device(k))

    def scan(r):
        def arrived(i):
            k = chip_peer(i)
            for u in range(per):
                remote(sums[r].at[k * per + u, pl.ds(0, ROWS[r])], in_piece(r, k, u),
                       s_in.at[r, k * per + u], r_in.at[r, k * per + u],
                       chip_device(k)).wait_recv()

        loop(chips - 1, arrived)

        def piece(u):
            def turn(i, run):
                k = i if r == 0 else chips - 1 - i
                outbox[r][k, u] = run
                drop = in_up[k, u, 64:72, :]
                one, two = (drop[0:1], drop[1:2]) if r == 0 else (drop[1:2], drop[0:1])
                return (jnp.concatenate([one * run[0:32], two * run[32:64]], axis=0)
                        + inbox[r][k, u, 0:64, :])

            lax.fori_loop(0, chips, turn, jnp.zeros((64, 128), F32))

        loop(per, piece)
        loop(chips - 1, lambda i: to_chip(r, chip_peer(i)).start())
        came[r][chip] = outbox[r][chip]

    loop(EARLY, inner)
    scan(0)
    loop(G, inner, EARLY)
    scan(1)

    sig_f = jnp.sum(bcf[:, :N] * bcf[:, N:], axis=1, keepdims=True)
    sig_r = jnp.sum(bcr[:, :N] * bcr[:, N:], axis=1, keepdims=True)
    sigma = jnp.where(lane < H, sig_f, jnp.where(lane < 2 * H, sig_r, 0.0))
    coef3 = jnp.concatenate(split3(sigma * step + skip), axis=1)

    def left3(a):
        hi, lo = split2(a)
        return jnp.concatenate([hi, lo, hi], axis=1)

    l_bf, l_cf = left3(bcf[:, :N]), left3(bcf[:, N:])
    l_br, l_cr = left3(bcr[:, :N]), left3(bcr[:, N:])

    def group_of(i):
        return lax.rem(chip * per // 2 + i, 8)

    def hand(g):
        spot = pl.ds(2 * g, 2)
        return remote(give.at[spot], carried.at[core, spot], s_hand.at[g], r_hand.at[g], partner)

    def receive(i):
        g = group_of(i)
        for n in range(2):
            p = 2 * g + n
            k = p // per
            for r in range(2):
                @pl.when((k != chip) & (p % per == 0))
                def _():
                    remote(outbox[r].at[k], came[r].at[k], s_out.at[r, k], r_out.at[r, k],
                           chip_device(k)).wait_recv()

                drops = drop_rows(r, p)
                for s in range(2):
                    rows = slice(32 * s, 32 * s + 32)
                    to = slice(64 * r + 32 * s, 64 * r + 32 * s + 32)
                    dm, dt = drops[s]
                    got = came[r][k, p % per, rows, :]
                    mine = pack[r][core, p, rows, :]
                    theirs = other[r][p, rows, :]
                    carried[core, p, to, :] = jnp.where(first[r], got, dt * got + theirs)
                    give[p, to, :] = jnp.where(first[r], dm * got + mine, got)
        hand(g).start()

    def work(i):
        g = group_of(i)
        remote(give.at[pl.ds(2 * g, 2)], carried.at[1 - core, pl.ds(2 * g, 2)],
               s_hand.at[g], r_hand.at[g], partner).wait_recv()
        groups = (8 * core + g, 8 * (1 - core) + g)
        places = [pl.ds(pl.multiple_of(j * 128, 128), 128) for j in groups]

        def wide(ref):
            return jnp.concatenate([ref[:, p] for p in places], axis=1)

        def state(s):
            rows = slice(32 * s, 32 * s + 32)
            return jnp.concatenate(
                [jnp.concatenate([carried[h, 2 * g, rows, :], carried[h, 2 * g + 1, rows, :]], axis=0)
                 for h in (core, 1 - core)], axis=1)

        state_f, adj_r, state_r, adj_f = state(0), state(1), state(2), state(3)
        sel_f, sel_r = spread(*groups)
        two_f, two_r = twice(sel_f), twice(sel_r)
        ef, er = mat(e2, two_f), mat(e2, two_r)
        tf, tr = mat(tail2, two_f), mat(tail2, two_r)
        one = sel_f + sel_r
        coef = mat(coef3, jnp.concatenate([one, one, one], axis=0))
        xj = wide(x_ref).astype(F32)
        dj = wide(dy_ref).astype(F32)
        wf, wr = tf * xj, tr * xj
        cuts = [split2(a) for a in (state_f, state_r, adj_f, adj_r)]

        def times(left, cut):
            return mat(left, jnp.concatenate([cut[0], cut[0], cut[1]], axis=0))

        yf = ef * times(l_cf, cuts[0])
        yr = er * times(l_cr, cuts[1])
        vf = times(l_bf, cuts[2])
        vr = times(l_br, cuts[3])
        out = wide(y_in) + (yf + yr) + coef * xj
        more = wide(dx) + (tf * vf + tr * vr) + coef * dj
        for n, p in enumerate(places):
            mixed_ref[:, p] = out[:, 128 * n : 128 * n + 128].astype(BF16)
            dx[:, p] = more[:, 128 * n : 128 * n + 128]
        back_f = sel_f.astype(F32).T.astype(BF16)
        back_r = sel_r.astype(F32).T.astype(BF16)
        rho[...] += mat2(dj * yf, back_f) + mat2(dj * yr, back_r)
        kap[...] += mat2(wf * vf, back_f) + mat2(wr * vr, back_r)
        in_f = jnp.sum(state_f * adj_f, axis=0, keepdims=True)
        in_r = jnp.sum(state_r * adj_r, axis=0, keepdims=True)
        omega[...] += (exact_right(jnp.broadcast_to(in_f, (8, 256)), back_f)
                       + exact_right(jnp.broadcast_to(in_r, (8, 256)), back_r))
        for n, (left, cut) in enumerate(zip((ef * dj, er * dj, wf, wr), cuts)):
            hi, lo = split2(left)
            acc[n] += mat_nt(hi, jnp.concatenate(cut, axis=0))
            accl[n] += mat_nt(lo, cut[0])

    def arrive(i):
        @pl.when(i < 8)
        def _():
            receive(i)

        @pl.when(i > 0)
        def _():
            work(i - 1)

    loop(9, arrive)

    def total(n):
        a = acc[n]
        return a[:, :N] + a[:, N:] + accl[n]

    colsum = cs[...].T
    kappa = kap[...]
    through = rs[...] - colsum + rho[...]
    d_fall = jnp.where(
        lane < H,
        exact_left(ones_where(row <= col), through) + exact_left(ones_where(row > col), kappa),
        exact_left(ones_where(row >= col), through) + exact_left(ones_where(row < col), kappa),
    ) + omega[0:1, :] * jnp.exp(last)
    small = jnp.exp(-jnp.abs(z))
    soft = jnp.maximum(z, 0.0) + jnp.log1p(small)
    sigmoid = jnp.where(z >= 0.0, 1.0, small) / (1.0 + small)
    ratio = jnp.where(z < -30.0, 1.0, sigmoid / jnp.maximum(soft, 1e-30))
    ksi = xi[...]
    diag = step * ksi
    straight = colsum + kappa + sigma * diag
    dz = straight * ratio - rate * d_fall * sigmoid * keep
    dz = jnp.where(lane < 2 * H, dz, 0.0)

    ds_f = jnp.sum(jnp.where(lane < H, diag, 0.0), axis=1, keepdims=True)
    ds_r = jnp.sum(jnp.where((lane >= H) & (lane < 2 * H), diag, 0.0), axis=1, keepdims=True)
    mixing = dsc[...]
    turned = mixing.T
    eq = row == col
    m_f = jnp.where(eq, ds_f, jnp.where(row > col, mixing, 0.0))
    m_r = jnp.where(eq, ds_r, jnp.where(row < col, mixing, 0.0))
    mt_f = jnp.where(eq, ds_f, jnp.where(row < col, turned, 0.0))
    mt_r = jnp.where(eq, ds_r, jnp.where(row > col, turned, 0.0))
    d_bcf = jnp.concatenate([total(2) + mat3(mt_f, bcf[:, N:]), total(0) + mat3(m_f, bcf[:, :N])], axis=1)
    d_bcr = jnp.concatenate([total(3) + mat3(mt_r, bcr[:, N:]), total(1) + mat3(m_r, bcr[:, :N])], axis=1)
    dproj = jnp.concatenate([dz, d_bcf, d_bcr], axis=1)
    p_hi, p_lo = split2(dproj)
    p_cat = jnp.concatenate([p_hi, p_lo, p_hi], axis=1)

    r128 = iota((128, 128), 0)
    c128 = iota((128, 128), 1)
    fold = ones_where(((r128 < H) & (r128 == c128))
                      | ((r128 >= H) & (r128 < 2 * H) & (r128 + c128 == 2 * H - 1)))
    vectors = jnp.concatenate(
        [jnp.sum(dz, axis=0, keepdims=True),
         -jnp.sum(step * d_fall, axis=0, keepdims=True),
         jnp.sum(ksi, axis=0, keepdims=True),
         jnp.zeros((5, 128), F32)], axis=0)
    dz_t = dz.T
    f_t = jnp.concatenate([dz_t[0:H], d_bcf.T], axis=0)
    r_hi, r_lo = split2(jnp.concatenate([dz_t[H : 2 * H], d_bcr.T], axis=0))
    f_hi, f_lo = split2(f_t)

    def ordered(a):
        return jnp.concatenate([mat(rev, a[0:H]).astype(BF16), a[H:]], axis=0)

    left = jnp.concatenate(
        [jnp.concatenate([f_hi, ordered(r_hi)], axis=1),
         jnp.concatenate([f_lo, ordered(r_lo)], axis=1)], axis=0)

    def tile(n):
        return (n // tiles, n % tiles)

    def weights(j):
        i = lax.rem(j + (W // 2) * (1 - core), W)
        cols = pl.ds(pl.multiple_of(i * 256, 256), 256)
        far = pl.ds(pl.multiple_of((W - 1 - i) * 256, 256), 256)
        right = jnp.concatenate(
            [x_ref[:, cols], mat(x_ref[:, far], flip).astype(BF16)], axis=0)
        got = mat(left, right)
        got = got[0:160] + got[160:320]
        for n in range(2):
            for m in range(TILES):
                a, b = tile((2 * i + n) * TILES + m)
                grad[a, b] = got[8 * m : 8 * m + 8, 128 * n : 128 * n + 128]

    def blank(n):
        a, b = tile(n)
        grad[a, b] = jnp.zeros((8, 128), F32)

    loop(2 * plane * tiles, blank, TILES * G + 1)
    a, b = tile(TILES * G)
    grad[a, b] = exact_right(vectors, fold)

    def core_copy(k):
        return remote(grad.at[(1 - core) * plane + k], from_core.at[k],
                      s_core.at[k], r_core.at[k], partner)

    def plane_copy(k):
        return remote(held.at[k], from_plane.at[p_me], s_plane.at[k], r_plane.at[p_me],
                      plane_device(k))

    loop(W // 2 + 1, weights)
    loop(plane, lambda i: core_copy(plane_peer(i)).start())
    loop(W, weights, W // 2 + 1)

    def add_core(i):
        k = plane_peer(i)
        core_copy(k).wait_recv()
        held[k] = grad[core * plane + k] + from_core[k]

    def forward(i):
        add_core(i)
        plane_copy(plane_peer(i)).start()

    loop(plane - 1, forward)
    add_core(plane - 1)

    def sequence(i):
        cols = pl.ds(pl.multiple_of(i * 256, 256), 256)
        w_hi = whi[:, cols]
        w_cat = jnp.concatenate([w_hi, w_hi, wlo[:, cols]], axis=0)
        dseq_ref[:, cols] = (dx[:, cols] + mat(p_cat, w_cat)).astype(BF16)

    loop(W, sequence)
    part[...] = jnp.zeros(part.shape, F32)
    part[0:tiles] = held[p_me]

    def add_plane(i):
        k = lax.rem(p_me + plane - 1 - i, plane)
        remote(held.at[k], from_plane.at[k], s_plane.at[k], r_plane.at[k],
               plane_device(k)).wait_recv()
        part[0:tiles] += from_plane[k]

    loop(plane - 1, add_plane)

    def z_span(k):
        return pl.ds(k * zt, zt)

    def z_copy(k):
        return remote(part.at[z_span(k)], from_z.at[z_me], s_z.at[k], r_z.at[z_me], z_device(k))

    loop(depth - 1, lambda i: z_copy(z_peer(i)).start())
    full[z_span(z_me)] = part[z_span(z_me)]

    def add_z(i):
        k = z_peer(i)
        remote(part.at[z_span(k)], from_z.at[k], s_z.at[k], r_z.at[k], z_device(k)).wait_recv()
        full[z_span(z_me)] += from_z[k]

    loop(depth - 1, add_z)

    def z_share(k):
        return remote(full.at[z_span(z_me)], full.at[z_span(z_me)],
                      s_zg.at[k], r_zg.at[z_me], z_device(k))

    loop(depth - 1, lambda i: z_share(z_peer(i)).start())

    def z_got(i):
        k = z_peer(i)
        remote(full.at[z_span(k)], full.at[z_span(k)],
               s_zg.at[k], r_zg.at[k], z_device(k)).wait_recv()

    loop(depth - 1, z_got)
    mine = core * plane + p_me
    all_ref[mine] = full[0:tiles]

    def plane_share(k):
        return remote(all_ref.at[mine], all_ref.at[mine], s_pg.at[k], r_pg.at[p_me],
                      plane_device(k))

    def core_share(k):
        spot = all_ref.at[core * plane + k]
        return remote(spot, spot, s_cg.at[k], r_cg.at[k], partner)

    loop(plane - 1, lambda i: plane_share(plane_peer(i)).start())
    core_share(p_me).start()

    def plane_got(i):
        k = lax.rem(p_me + plane - 1 - i, plane)
        spot = all_ref.at[core * plane + k]
        remote(spot, spot, s_pg.at[k], r_pg.at[k], plane_device(k)).wait_recv()
        core_share(k).start()

    loop(plane - 1, plane_got)

    def core_got(k):
        spot = all_ref.at[(1 - core) * plane + k]
        remote(spot, spot, s_cg.at[k], r_cg.at[k], partner).wait_recv()

    loop(plane, core_got)

    def unpack(j):
        cols = pl.ds(pl.multiple_of(j * 128, 128), 128)
        for m in range(TILES):
            ref, base = (dt_ref, 0) if m < 4 else (b_ref, 4) if m < 12 else (c_ref, 12)
            a, b = tile(j * TILES + m)
            ref[8 * (m - base) : 8 * (m - base) + 8, cols] = all_ref[a, b]

    loop(G, unpack)
    a, b = tile(TILES * G)
    vec_ref[...] = all_ref[a, b]

    for r in range(2):
        loop(4, lambda q, r=r: swap(r, q).wait_send())
        loop(chips - 1, lambda i, r=r: to_chip(r, chip_peer(i)).wait_send())
        loop(PIECES - per, lambda i, r=r: to_owner(
            r, lax.rem((chip + 1) * per + i, PIECES)).wait_send())
    loop(8, lambda g: hand(g).wait_send())
    loop(plane, lambda k: core_copy(k).wait_send())
    loop(plane, lambda k: core_share(k).wait_send())
    loop(plane - 1, lambda i: plane_copy(plane_peer(i)).wait_send())
    loop(plane - 1, lambda i: plane_share(plane_peer(i)).wait_send())
    loop(depth - 1, lambda i: z_copy(z_peer(i)).wait_send())
    loop(depth - 1, lambda i: z_share(z_peer(i)).wait_send())


def sds(shape, dtype=F32):
    return jax.ShapeDtypeStruct(shape, dtype)


def on_device(sizes, sequence, n_blocks, w_dt, dt_bias, decay_rate, w_b, w_c, d_skip, cotangent):
    dps, ctxs = sizes
    chips = ctxs // 2
    halves = 2 if ctxs % 4 == 0 else 1
    depth = chips // halves
    plane = dps * halves
    tiles = -(-(TILES * G + 1) // (2 * plane))
    zt = -(-tiles // depth)
    per = PIECES // chips
    dma = pltpu.SemaphoreType.DMA

    def mem(*shape, dtype=F32):
        return pltpu.VMEM(shape, dtype)

    up, down = ROWS
    mixed, dseq, grad_dt, grad_b, grad_c, vectors = pl.pallas_call(
        functools.partial(kernel, chips, halves, depth),
        out_shape=[sds((T, D), BF16), sds((T, D), BF16),
                   sds((H, D)), sds((N, D)), sds((N, D)), sds((8, 128))],
        in_specs=[VMEM, VMEM, SMEM] + [VMEM] * 6,
        out_specs=[VMEM] * 6,
        scratch_shapes=[
            mem(384, D, dtype=BF16), mem(384, D, dtype=BF16), mem(128, T),
            mem(T, D), mem(T, D), mem(T, T), mem(T, 128), mem(128, T), mem(T, 128),
            mem(T, T), mem(T, 384, dtype=BF16),
            mem(T, 128), mem(T, 128), mem(8, 128), mem(4, T, 128), mem(4, T, N),
            mem(2, PIECES, up, 128), mem(2, PIECES, down, 128),
            mem(PIECES, up, 128), mem(PIECES, down, 128),
            mem(PIECES, up, 128), mem(PIECES, down, 128),
            mem(chips, per, up, 128), mem(chips, per, down, 128),
            mem(chips, per, 64, 128), mem(chips, per, 64, 128),
            mem(chips, per, 64, 128), mem(chips, per, 64, 128),
            mem(PIECES, 128, 128), mem(2, PIECES, 128, 128),
            mem(2 * plane, tiles, 8, 128), mem(2 * plane, tiles, 8, 128),
            mem(plane, tiles, 8, 128), mem(plane, tiles, 8, 128), mem(plane, tiles, 8, 128),
            mem(depth * zt, 8, 128), mem(depth, zt, 8, 128), mem(depth * zt, 8, 128),
            dma((2, 4)), dma((2, 4)), dma((2, PIECES)), dma((2, PIECES)),
            dma((2, chips)), dma((2, chips)), dma((8,)), dma((8,)),
        ] + [dma((plane,))] * 4 + [dma((depth,))] * 4 + [dma((plane,))] * 4,
        compiler_params=pltpu.CompilerParams(
            vmem_limit_bytes=ALL, collective_id=0, has_side_effects=True),
    )(sequence[0], cotangent[0], n_blocks, w_dt.T, w_b.T, w_c.T,
      dt_bias[None], decay_rate[None], d_skip[None])

    return (mixed[None], dseq[None], grad_dt.T, vectors[0, :H], vectors[1, :H],
            grad_b.T, grad_c.T, vectors[2, :H])


def solution(mesh):
    sizes = (mesh.shape["dp"], mesh.shape["ctx"])
    return jax.shard_map(
        functools.partial(on_device, sizes),
        mesh=mesh,
        in_specs=(
            P("dp", "ctx", None),
            P("dp", "ctx"),
            P(), P(), P(), P(), P(), P(),
            P("dp", "ctx", None),
        ),
        out_specs=(P("dp", "ctx", None), P("dp", "ctx", None), P(), P(), P(), P(), P(), P()),
        check_vma=False,
    )
```

```python
import functools

import jax
import jax.numpy as jnp
from jax import lax
from jax.experimental import pallas as pl
from jax.experimental.pallas import tpu as pltpu
from jax.sharding import PartitionSpec as P

F32 = jnp.float32
BF16 = jnp.bfloat16
BLOCK = 128
T = 256
D = 2048
H = 32
N = 64
G = 16
W = D // 256
MESH = pl.DeviceIdType.MESH
VMEM = pl.BlockSpec(memory_space=pltpu.VMEM)
SMEM = pl.BlockSpec(memory_space=pltpu.SMEM)
ALL = 62 * 1024 * 1024
PIECES = 16
ROWS = (72, 64)
TILES = 20
FAR = -1e30
EARLY, LATER = 10, 13


def iota(shape, axis):
    return lax.broadcasted_iota(jnp.int32, shape, axis)


def mat(a, b):
    return lax.dot_general(a, b, (((1,), (0,)), ((), ())), preferred_element_type=F32)


def mat_nt(a, b):
    return lax.dot_general(a, b, (((1,), (1,)), ((), ())), preferred_element_type=F32)


def split2(a):
    hi = a.astype(BF16)
    return hi, (a - hi.astype(F32)).astype(BF16)


def split3(a):
    hi = a.astype(BF16)
    rest = a - hi.astype(F32)
    mid = rest.astype(BF16)
    return hi, mid, (rest - mid.astype(F32)).astype(BF16)


def mat2(a, exact):
    hi, lo = split2(a)
    return mat(hi, exact) + mat(lo, exact)


def mat3(a, b):
    ah, al = split2(a)
    bh, bl = split2(b)
    return mat(ah, bh) + (mat(al, bh) + mat(ah, bl))


def mat3_nt(a, b):
    ah, al = split2(a)
    bh, bl = split2(b)
    return mat_nt(ah, bh) + (mat_nt(al, bh) + mat_nt(ah, bl))


def exact_left(zero_one, a):
    hi, mid, lo = split3(a)
    return mat(zero_one, hi) + (mat(zero_one, mid) + mat(zero_one, lo))


def exact_right(a, zero_one):
    hi, mid, lo = split3(a)
    return mat(hi, zero_one) + (mat(mid, zero_one) + mat(lo, zero_one))


def ones_where(condition):
    return jnp.where(condition, 1.0, 0.0).astype(BF16)


def backwards(size):
    return ones_where(iota((size, size), 0) + iota((size, size), 1) == size - 1)


def keep_column(nb_ref):
    first = 1.0 - nb_ref[0, 0].astype(F32)
    second = 1.0 - nb_ref[0, 1].astype(F32)
    return jnp.where(iota((T, 1), 0) < BLOCK, first, second)


def spread(first, second):
    rows = iota((128, 256), 0)
    cols = iota((128, 256), 1)
    head = jnp.where(cols < 128, 2 * first, 2 * second) + (cols % 128) // N
    return ones_where(rows == head), ones_where(rows == head + H)


def twice(a):
    return jnp.concatenate([a, a], axis=0)


def lanes2(a):
    return jnp.concatenate(split2(a), axis=1)


def inner_setup(c, bcf, bcr, sc, c3, dsc):
    row = iota((T, T), 0)
    col = iota((T, T), 1)
    sf = mat3_nt(bcf[:, N:], bcf[:, :N])
    sr = mat3_nt(bcr[:, N:], bcr[:, :N])
    sc[...] = jnp.where(row > col, sf, jnp.where(row < col, sr, 0.0))
    c3[...] = jnp.concatenate(split3(c), axis=1)
    dsc[...] = jnp.zeros((T, T), F32)


def inner_pair(i, x_ref, dy_ref, at_ref, sc, c3, y_ref, dx_ref, dsc, rs_ref, cs_ref, xi_ref):
    cols = pl.ds(pl.multiple_of(i * 128, 128), 128)
    xp = x_ref[:, cols]
    dp = dy_ref[:, cols]
    dpt = dp.astype(F32).T.astype(BF16)
    seg_rows = iota((128, 128), 0) // N + 2 * i
    seg_cols = iota((128, 128), 1)
    seg = ones_where((seg_cols < 2 * H) & (seg_cols % H == seg_rows))
    xi_ref[...] += mat2(dp.astype(F32) * xp.astype(F32), seg)
    lane = iota((1, 128), 1)
    row = iota((BLOCK, BLOCK), 0)
    col = iota((BLOCK, BLOCK), 1)
    low = row > col
    up = row < col
    lanes = iota((T, 128), 1)
    y = jnp.zeros((T, 128), F32)
    dut = []
    for k in range(2):
        h = 2 * i + k
        mask = ones_where((lane // N) == k)
        xm = xp * mask
        cross = mat_nt(dp * mask, xp)
        rows3 = iota((384, T), 0) % 128
        cols3 = iota((384, T), 1)
        sel = ones_where(rows3 == h + jnp.where(cols3 < 128, 0, H))
        cb = mat(c3[...], sel)
        af = at_ref[pl.ds(h, 1), :]
        ar = at_ref[pl.ds(H + h, 1), :]
        top = slice(0, BLOCK)
        bot = slice(BLOCK, T)

        def args(rows, columns):
            forward = cb[rows, 0:128] + af[:, columns]
            reverse = cb[rows, 128:256] + ar[:, columns]
            return forward, reverse

        e = {}
        for r in (top, bot):
            for q in (top, bot):
                f, b = args(r, q)
                if r is q:
                    arg = jnp.where(low, f, jnp.where(up, b, FAR))
                else:
                    arg = f if r is bot else b
                e[r is bot, q is bot] = jnp.exp(arg)
        kk = {}
        g = {}
        for r in (top, bot):
            for q in (top, bot):
                key = (r is bot, q is bot)
                kk[key] = sc[r, q] * e[key]
                xx = cross[r, q]
                g[key] = xx * kk[key]
                dsc[r, q] += xx * e[key]
        g0f = jnp.where(low, g[False, False], 0.0)
        g0r = g[False, False] - g0f
        g1f = jnp.where(low, g[True, True], 0.0)
        g1r = g[True, True] - g1f
        rf = jnp.concatenate(
            [jnp.sum(g0f, axis=1, keepdims=True),
             jnp.sum(g[True, False] + g1f, axis=1, keepdims=True)], axis=0)
        rr = jnp.concatenate(
            [jnp.sum(g0r + g[False, True], axis=1, keepdims=True),
             jnp.sum(g1r, axis=1, keepdims=True)], axis=0)
        rs_ref[...] = jnp.where(lanes == h, rf, jnp.where(lanes == H + h, rr, rs_ref[...]))
        cs_ref[pl.ds(h, 1), :] = jnp.concatenate(
            [jnp.sum(g0f + g[True, False], axis=0, keepdims=True),
             jnp.sum(g1f, axis=0, keepdims=True)], axis=1)
        cs_ref[pl.ds(H + h, 1), :] = jnp.concatenate(
            [jnp.sum(g0r, axis=0, keepdims=True),
             jnp.sum(g[False, True] + g1r, axis=0, keepdims=True)], axis=1)
        full = jnp.concatenate(
            [jnp.concatenate([kk[False, False], kk[False, True]], axis=1),
             jnp.concatenate([kk[True, False], kk[True, True]], axis=1)], axis=0)
        hi, lo = split2(full)
        y = y + mat(hi, xm) + mat(lo, xm)
        rows = dpt[N * k : N * (k + 1), :]
        dut.append(mat(rows, hi) + mat(rows, lo))
    y_ref[:, cols] = y
    dx_ref[:, cols] = jnp.concatenate(dut, axis=0).T


def kernel(halves, depth, x_ref, dy_ref, nb_ref, wdt_ref, wb_ref, wc_ref,
           bias_ref, rate_ref, skip_ref,
           mixed_ref, dseq_ref, dt_ref, b_ref, c_ref, vec_ref,
           whi, wlo, at_ref, y_in, dx, dsc, rs, cs, xi, sc, c3, rho, kap, omega, acc, accl,
           pack_up, pack_down, other_up, other_down, sums_up, sums_down, in_up, in_down,
           out_up, out_down, came_up, came_down, give, carried, whole, begin,
           grad, all_ref, from_core, held, from_plane, part, from_z, full,
           s_swap, r_swap, s_in, r_in, s_out, r_out, s_half, r_half, s_hand, r_hand,
           s_core, r_core, s_plane, r_plane, s_z, r_z, s_zg, r_zg, s_pg, r_pg, s_cg, r_cg):
    per = PIECES // depth
    pack, other = (pack_up, pack_down), (other_up, other_down)
    sums, inbox = (sums_up, sums_down), (in_up, in_down)
    outbox, came = (out_up, out_down), (came_up, came_down)
    plane = held.shape[0]
    tiles = held.shape[1]
    zt = from_z.shape[1]
    dp = lax.axis_index("dp")
    ctx = lax.axis_index("ctx")
    core = ctx % 2
    chip = ctx // 2
    z_me = chip % depth
    half_me = chip // depth
    p_me = dp * halves + half_me
    partner = (dp, ctx + 1 - 2 * core)

    def plane_device(k):
        return (k // halves, ((k % halves) * depth + z_me) * 2 + core)

    def plane_peer(i):
        return lax.rem(p_me + 1 + i, plane)

    def z_device(k):
        return (dp, (half_me * depth + k) * 2 + core)

    def z_peer(i):
        return lax.rem(z_me + 1 + i, depth)

    def remote(src, dst, send, recv, device):
        return pltpu.make_async_remote_copy(
            src_ref=src, dst_ref=dst, send_sem=send, recv_sem=recv,
            device_id=device, device_id_type=MESH,
        )

    def loop(count, body, start=0):
        def step(i, carry):
            body(i)
            return carry

        lax.fori_loop(start, count, step, 0)

    barrier = pltpu.get_barrier_semaphore()
    pl.semaphore_signal(barrier, inc=1, device_id=partner, device_id_type=MESH)
    loop(depth - 1, lambda i: pl.semaphore_signal(
        barrier, inc=1, device_id=z_device(z_peer(i)), device_id_type=MESH))
    loop(plane - 1, lambda i: pl.semaphore_signal(
        barrier, inc=1, device_id=plane_device(plane_peer(i)), device_id_type=MESH))

    flip = backwards(256)
    rev = backwards(H)
    both = ones_where((iota((H, 128), 1) == iota((H, 128), 0))
                      | (iota((H, 128), 1) + iota((H, 128), 0) == 2 * H - 1))
    bias, rate, skip = (
        exact_right(jnp.broadcast_to(ref[...], (8, H)), both)[0:1]
        for ref in (bias_ref, rate_ref, skip_ref)
    )

    def cut(i, carry):
        here = pl.ds(pl.multiple_of(i * 256, 256), 256)
        there = pl.ds(pl.multiple_of((W - 1 - i) * 256, 256), 256)
        raw = jnp.concatenate([wdt_ref[:, here], wb_ref[:, here], wc_ref[:, here]], axis=0)
        hi, lo = split2(raw)
        turned = mat(jnp.concatenate([hi, lo], axis=0), flip).astype(BF16)
        for ref, own, far in ((whi, hi, turned[0:160]), (wlo, lo, turned[160:320])):
            ref[0:H, here] = own[0:H]
            ref[128:256, here] = own[H:160]
            ref[H : 2 * H, there] = mat(rev, far[0:H]).astype(BF16)
            ref[256:384, there] = far[H:160]
            ref[2 * H : 128, here] = jnp.zeros((2 * H, 256), BF16)
        return carry

    lax.fori_loop(0, W, cut, 0, unroll=2)

    x = x_ref[...]
    proj = mat_nt(x, whi[...]) + mat_nt(x, wlo[...])
    lane = iota((T, 128), 1)
    row = iota((T, T), 0)
    col = iota((T, T), 1)
    keep = keep_column(nb_ref)
    z = proj[:, 0:128] + bias
    soft = jnp.maximum(z, 0.0) + jnp.log1p(jnp.exp(-jnp.abs(z)))
    step = jnp.where(lane < 2 * H, soft * keep, 0.0)
    fall = -step * rate
    c = jnp.where(
        lane < H,
        exact_left(ones_where(row >= col), fall),
        exact_left(ones_where(row <= col), fall),
    )
    last = jnp.where(lane[0:1] < H, c[T - 1 : T], c[0:1])
    at_ref[...] = jnp.where(step > 0.0, jnp.log(jnp.maximum(step, 1e-37)) - c, FAR).T
    bcf = proj[:, 128:256]
    bcr = proj[:, 256:384]
    e2 = lanes2(jnp.exp(c))
    tail2 = lanes2(jnp.exp(last - c) * step)
    decay8 = jnp.broadcast_to(jnp.exp(last), (8, 128))
    tf_hi, tf_lo = split2(bcf.T)
    tr_hi, tr_lo = split2(bcr.T)

    lefts = [
        jnp.concatenate([hi[span], lo[span]], axis=0)
        for hi, lo, span in (
            (tf_hi, tf_lo, slice(0, N)),
            (tr_hi, tr_lo, slice(N, 2 * N)),
            (tr_hi, tr_lo, slice(0, N)),
            (tf_hi, tf_lo, slice(N, 2 * N)),
        )
    ]
    first = (core == 0, core == 1)

    def block(i):
        return lax.rem(i + z_me * per // 4, 4)

    def swap(r, q):
        spot = pl.ds(4 * q, 4)
        return remote(pack[r].at[1 - core, spot], other[r].at[spot],
                      s_swap.at[r, q], r_swap.at[r, q], partner)

    def slot(k, g):
        return k * (per // 2) + g % (per // 2)

    def to_owner(r, g):
        return remote(sums[r].at[pl.ds(2 * g, 2), pl.ds(0, ROWS[r])],
                      inbox[r].at[z_me, pl.ds(2 * g % per, 2)],
                      s_in.at[r, g], r_in.at[r, slot(z_me, g)], z_device(2 * g // per))

    def local_states(r, half, q):
        i = 4 * half + q
        cols = pl.ds(pl.multiple_of(i * 256, 256), 256)
        sel_f, sel_r = spread(2 * i, 2 * i + 1)
        two_f, two_r = twice(sel_f), twice(sel_r)
        xj = x_ref[:, cols].astype(F32)
        dj = dy_ref[:, cols].astype(F32)
        if r == 0:
            rights = mat(tail2, two_f) * xj, mat(e2, two_r) * dj
            drops = jnp.where(iota((8, 256), 0) == 0,
                              exact_right(decay8, sel_f), exact_right(decay8, sel_r))
        else:
            rights = mat(tail2, two_r) * xj, mat(e2, two_f) * dj
        for s in range(2):
            left = lefts[2 * r + s]
            hi, lo = split2(rights[s])
            wide = mat(left, hi)
            got = wide[0:N] + wide[N : 2 * N] + mat(left[0:N], lo)
            for g in range(2):
                lanes = slice(128 * g, 128 * g + 128)
                for h in range(2):
                    p = 4 * q + 2 * g + h
                    pack[r][half, p, 32 * s : 32 * s + 32, :] = got[32 * h : 32 * h + 32, lanes]
                    if r == 0 and s == 0:
                        pack[r][half, p, 64:72, :] = drops[:, lanes]

    def drop_rows(r, p):
        mine = pack_up[core, p, 64:72, :]
        theirs = other_up[p, 64:72, :]
        order = (0, 1) if r == 0 else (1, 0)
        return [(mine[n : n + 1], theirs[n : n + 1]) for n in order]

    def add_up(r, q):
        swap(r, q).wait_recv()
        for n in range(2):
            g = 2 * q + n
            own = 2 * g // per == z_me
            both_pieces = []
            for p in (2 * g, 2 * g + 1):
                drops = drop_rows(r, p)
                out = []
                for s in range(2):
                    rows = slice(32 * s, 32 * s + 32)
                    dm, dt = drops[s]
                    mine = pack[r][core, p, rows, :]
                    theirs = other[r][p, rows, :]
                    out.append(jnp.where(first[r], dt * mine + theirs, dm * theirs + mine))
                if r == 0:
                    out.append(pack_up[core, p, 64:72, :] * other_up[p, 64:72, :])
                both_pieces.append(jnp.concatenate(out, axis=0))

            @pl.when(own)
            def _():
                for h in range(2):
                    inbox[r][z_me, 2 * g % per + h] = both_pieces[h]

            @pl.when(jnp.logical_not(own))
            def _():
                for h in range(2):
                    sums[r][2 * g + h] = both_pieces[h]
                to_owner(r, g).start()

    pl.semaphore_wait(barrier, plane + depth - 1)
    for r in range(2):
        def states(i, r=r):
            @pl.when(i < 4)
            def _():
                q = block(i)
                local_states(r, 1 - core, q)
                swap(r, q).start()
                local_states(r, core, q)

            @pl.when(i > 0)
            def _():
                add_up(r, block(i - 1))

        loop(5, states)

    inner_setup(c, bcf, bcr, sc, c3, dsc)
    rs[...] = jnp.zeros((T, 128), F32)
    cs[...] = jnp.zeros((128, T), F32)
    xi[...] = jnp.zeros((T, 128), F32)
    for ref in (rho, kap, omega, acc, accl):
        ref[...] = jnp.zeros(ref.shape, F32)

    def inner(i):
        inner_pair(i, x_ref, dy_ref, at_ref, sc, c3, y_in, dx, dsc, rs, cs, xi)

    def to_chip(r, k):
        return remote(outbox[r].at[k], came[r].at[z_me],
                      s_out.at[r, k], r_out.at[r, z_me], z_device(k))

    def across(r):
        return remote(whole.at[r], begin.at[r], s_half.at[r], r_half.at[r],
                      (dp, ((1 - half_me) * depth + z_me) * 2 + core))

    def scan(r):
        def piece(u):
            def turn(i, run):
                k = i if r == 0 else depth - 1 - i
                outbox[r][k, u] = run
                drop = in_up[k, u, 64:72, :]
                one, two = (drop[0:1], drop[1:2]) if r == 0 else (drop[1:2], drop[0:1])
                return (jnp.concatenate([one * run[0:32], two * run[32:64]], axis=0)
                        + inbox[r][k, u, 0:64, :])

            whole[r, u] = lax.fori_loop(0, depth, turn, begin[r, u])

        loop(per, piece)

    def scatter(r):
        loop(depth - 1, lambda i: to_chip(r, z_peer(i)).start())
        came[r][z_me] = outbox[r][z_me]

    def gives(r):
        return half_me == (0 if r == 0 else halves - 1)

    def collect(r):
        def arrived(i):
            k = z_peer(i)
            for n in range(per // 2):
                g = k * (per // 2) + n
                remote(sums[r].at[pl.ds(2 * g, 2), pl.ds(0, ROWS[r])],
                       inbox[r].at[k, pl.ds(2 * n, 2)],
                       s_in.at[r, g], r_in.at[r, g], z_device(k)).wait_recv()

        loop(depth - 1, arrived)

        @pl.when(gives(r))
        def _():
            begin[r] = jnp.zeros((per, 64, 128), F32)
            scan(r)
            if halves == 2:
                across(r).start()
            scatter(r)

    def finish(r):
        @pl.when(jnp.logical_not(gives(r)))
        def _():
            across(r).wait_recv()
            scan(r)
            scatter(r)

    loop(EARLY, inner)
    collect(0)
    loop(LATER, inner, EARLY)
    finish(0)
    loop(G, inner, LATER)
    collect(1)
    finish(1)

    sig_f = jnp.sum(bcf[:, :N] * bcf[:, N:], axis=1, keepdims=True)
    sig_r = jnp.sum(bcr[:, :N] * bcr[:, N:], axis=1, keepdims=True)
    sigma = jnp.where(lane < H, sig_f, jnp.where(lane < 2 * H, sig_r, 0.0))
    coef3 = jnp.concatenate(split3(sigma * step + skip), axis=1)

    def left3(a):
        hi, lo = split2(a)
        return jnp.concatenate([hi, lo, hi], axis=1)

    l_bf, l_cf = left3(bcf[:, :N]), left3(bcf[:, N:])
    l_br, l_cr = left3(bcr[:, :N]), left3(bcr[:, N:])

    def group_of(i):
        return lax.rem(z_me * per // 2 + i, 8)

    def hand(r, g):
        spot = pl.ds(2 * g, 2)
        rows = pl.ds(64 * r, 64)
        return remote(give.at[spot, rows], carried.at[core, spot, rows],
                      s_hand.at[r, g], r_hand.at[r, g], partner)

    def receive(r, i):
        g = group_of(i)
        k = 2 * g // per

        @pl.when((k != z_me) & (2 * g % per == 0))
        def _():
            remote(outbox[r].at[k], came[r].at[k], s_out.at[r, k], r_out.at[r, k],
                   z_device(k)).wait_recv()

        for p in (2 * g, 2 * g + 1):
            drops = drop_rows(r, p)
            for s in range(2):
                rows = slice(32 * s, 32 * s + 32)
                to = slice(64 * r + 32 * s, 64 * r + 32 * s + 32)
                dm, dt = drops[s]
                got = came[r][k, p % per, rows, :]
                mine = pack[r][core, p, rows, :]
                theirs = other[r][p, rows, :]
                carried[core, p, to, :] = jnp.where(first[r], got, dt * got + theirs)
                give[p, to, :] = jnp.where(first[r], dm * got + mine, got)
        hand(r, g).start()

    def work(r, i):
        g = group_of(i)
        spot = pl.ds(2 * g, 2)
        span = pl.ds(64 * r, 64)
        remote(give.at[spot, span], carried.at[1 - core, spot, span],
               s_hand.at[r, g], r_hand.at[r, g], partner).wait_recv()
        groups = (8 * core + g, 8 * (1 - core) + g)
        places = [pl.ds(pl.multiple_of(j * 128, 128), 128) for j in groups]

        def wide(ref):
            return jnp.concatenate([ref[:, p] for p in places], axis=1)

        def state(s):
            rows = slice(32 * s, 32 * s + 32)
            return jnp.concatenate(
                [jnp.concatenate([carried[h, 2 * g, rows, :], carried[h, 2 * g + 1, rows, :]], axis=0)
                 for h in (core, 1 - core)], axis=1)

        now, adj = state(2 * r), state(2 * r + 1)
        sel = spread(*groups)
        sel_s, sel_a = sel[r], sel[1 - r]
        e = mat(e2, twice(sel_s))
        t = mat(tail2, twice(sel_a))
        xj = wide(x_ref).astype(F32)
        dj = wide(dy_ref).astype(F32)
        w = t * xj
        cut_s, cut_a = split2(now), split2(adj)

        def times(left, cut):
            return mat(left, jnp.concatenate([cut[0], cut[0], cut[1]], axis=0))

        y = e * times((l_cf, l_cr)[r], cut_s)
        v = times((l_br, l_bf)[r], cut_a)
        out = wide(y_in) + y
        more = wide(dx) + t * v
        if r == 0:
            one = sel[0] + sel[1]
            coef = mat(coef3, jnp.concatenate([one, one, one], axis=0))
            out = out + coef * xj
            more = more + coef * dj
        for n, p in enumerate(places):
            part_out = out[:, 128 * n : 128 * n + 128]
            if r == 0:
                y_in[:, p] = part_out
            else:
                mixed_ref[:, p] = part_out.astype(BF16)
            dx[:, p] = more[:, 128 * n : 128 * n + 128]
        back = [a.astype(F32).T.astype(BF16) for a in sel]
        rho[...] += mat2(dj * y, back[r])
        kap[...] += mat2(w * v, back[1 - r])
        if r == 1:
            in_f = jnp.sum(state(0) * adj, axis=0, keepdims=True)
            in_r = jnp.sum(now * state(1), axis=0, keepdims=True)
            omega[...] += (exact_right(jnp.broadcast_to(in_f, (8, 256)), back[0])
                           + exact_right(jnp.broadcast_to(in_r, (8, 256)), back[1]))
        for n, left, cut in ((r, e * dj, cut_s), (3 - r, w, cut_a)):
            hi, lo = split2(left)
            acc[n] += mat_nt(hi, jnp.concatenate(cut, axis=0))
            accl[n] += mat_nt(lo, cut[0])

    for r in range(2):
        def arrive(i, r=r):
            @pl.when(i < 8)
            def _():
                receive(r, i)

            @pl.when(i > 0)
            def _():
                work(r, i - 1)

        loop(9, arrive)

    def total(n):
        a = acc[n]
        return a[:, :N] + a[:, N:] + accl[n]

    colsum = cs[...].T
    kappa = kap[...]
    through = rs[...] - colsum + rho[...]
    d_fall = jnp.where(
        lane < H,
        exact_left(ones_where(row <= col), through) + exact_left(ones_where(row > col), kappa),
        exact_left(ones_where(row >= col), through) + exact_left(ones_where(row < col), kappa),
    ) + omega[0:1, :] * jnp.exp(last)
    small = jnp.exp(-jnp.abs(z))
    soft = jnp.maximum(z, 0.0) + jnp.log1p(small)
    sigmoid = jnp.where(z >= 0.0, 1.0, small) / (1.0 + small)
    ratio = jnp.where(z < -30.0, 1.0, sigmoid / jnp.maximum(soft, 1e-30))
    ksi = xi[...]
    diag = step * ksi
    straight = colsum + kappa + sigma * diag
    dz = straight * ratio - rate * d_fall * sigmoid * keep
    dz = jnp.where(lane < 2 * H, dz, 0.0)

    ds_f = jnp.sum(jnp.where(lane < H, diag, 0.0), axis=1, keepdims=True)
    ds_r = jnp.sum(jnp.where((lane >= H) & (lane < 2 * H), diag, 0.0), axis=1, keepdims=True)
    mixing = dsc[...]
    turned = mixing.T
    eq = row == col
    m_f = jnp.where(eq, ds_f, jnp.where(row > col, mixing, 0.0))
    m_r = jnp.where(eq, ds_r, jnp.where(row < col, mixing, 0.0))
    mt_f = jnp.where(eq, ds_f, jnp.where(row < col, turned, 0.0))
    mt_r = jnp.where(eq, ds_r, jnp.where(row > col, turned, 0.0))
    d_bcf = jnp.concatenate([total(2) + mat3(mt_f, bcf[:, N:]), total(0) + mat3(m_f, bcf[:, :N])], axis=1)
    d_bcr = jnp.concatenate([total(3) + mat3(mt_r, bcr[:, N:]), total(1) + mat3(m_r, bcr[:, :N])], axis=1)
    dproj = jnp.concatenate([dz, d_bcf, d_bcr], axis=1)
    p_hi, p_lo = split2(dproj)
    p_cat = jnp.concatenate([p_hi, p_lo, p_hi], axis=1)

    r128 = iota((128, 128), 0)
    c128 = iota((128, 128), 1)
    fold = ones_where(((r128 < H) & (r128 == c128))
                      | ((r128 >= H) & (r128 < 2 * H) & (r128 + c128 == 2 * H - 1)))
    vectors = jnp.concatenate(
        [jnp.sum(dz, axis=0, keepdims=True),
         -jnp.sum(step * d_fall, axis=0, keepdims=True),
         jnp.sum(ksi, axis=0, keepdims=True),
         jnp.zeros((5, 128), F32)], axis=0)
    dz_t = dz.T
    f_t = jnp.concatenate([dz_t[0:H], d_bcf.T], axis=0)
    r_hi, r_lo = split2(jnp.concatenate([dz_t[H : 2 * H], d_bcr.T], axis=0))
    f_hi, f_lo = split2(f_t)

    def ordered(a):
        return jnp.concatenate([mat(rev, a[0:H]).astype(BF16), a[H:]], axis=0)

    left = jnp.concatenate(
        [jnp.concatenate([f_hi, ordered(r_hi)], axis=1),
         jnp.concatenate([f_lo, ordered(r_lo)], axis=1)], axis=0)

    def tile(n):
        return (n // tiles, n % tiles)

    def weights(j):
        i = lax.rem(j + (W // 2) * (1 - core), W)
        cols = pl.ds(pl.multiple_of(i * 256, 256), 256)
        far = pl.ds(pl.multiple_of((W - 1 - i) * 256, 256), 256)
        right = jnp.concatenate(
            [x_ref[:, cols], mat(x_ref[:, far], flip).astype(BF16)], axis=0)
        got = mat(left, right)
        got = got[0:160] + got[160:320]
        for n in range(2):
            for m in range(TILES):
                a, b = tile((2 * i + n) * TILES + m)
                grad[a, b] = got[8 * m : 8 * m + 8, 128 * n : 128 * n + 128]

    def blank(n):
        a, b = tile(n)
        grad[a, b] = jnp.zeros((8, 128), F32)

    loop(2 * plane * tiles, blank, TILES * G + 1)
    a, b = tile(TILES * G)
    grad[a, b] = exact_right(vectors, fold)

    def core_copy(k):
        return remote(grad.at[(1 - core) * plane + k], from_core.at[k],
                      s_core.at[k], r_core.at[k], partner)

    def plane_copy(k):
        return remote(held.at[k], from_plane.at[p_me], s_plane.at[k], r_plane.at[p_me],
                      plane_device(k))

    loop(W // 2 + 1, weights)
    loop(plane, lambda i: core_copy(plane_peer(i)).start())
    loop(W, weights, W // 2 + 1)

    def add_core(i):
        k = plane_peer(i)
        core_copy(k).wait_recv()
        held[k] = grad[core * plane + k] + from_core[k]

    def forward(i):
        add_core(i)
        plane_copy(plane_peer(i)).start()

    loop(plane - 1, forward)
    add_core(plane - 1)

    def sequence(i):
        cols = pl.ds(pl.multiple_of(i * 256, 256), 256)
        w_hi = whi[:, cols]
        w_cat = jnp.concatenate([w_hi, w_hi, wlo[:, cols]], axis=0)
        dseq_ref[:, cols] = (dx[:, cols] + mat(p_cat, w_cat)).astype(BF16)

    loop(W, sequence)
    part[...] = jnp.zeros(part.shape, F32)
    part[0:tiles] = held[p_me]

    def add_plane(i):
        k = lax.rem(p_me + plane - 1 - i, plane)
        remote(held.at[k], from_plane.at[k], s_plane.at[k], r_plane.at[k],
               plane_device(k)).wait_recv()
        part[0:tiles] += from_plane[k]

    loop(plane - 1, add_plane)

    def z_span(k):
        return pl.ds(k * zt, zt)

    def z_copy(k):
        return remote(part.at[z_span(k)], from_z.at[z_me], s_z.at[k], r_z.at[z_me], z_device(k))

    loop(depth - 1, lambda i: z_copy(z_peer(i)).start())
    full[z_span(z_me)] = part[z_span(z_me)]

    def add_z(i):
        k = z_peer(i)
        remote(part.at[z_span(k)], from_z.at[k], s_z.at[k], r_z.at[k], z_device(k)).wait_recv()
        full[z_span(z_me)] += from_z[k]

    loop(depth - 1, add_z)

    def z_share(k):
        return remote(full.at[z_span(z_me)], full.at[z_span(z_me)],
                      s_zg.at[k], r_zg.at[z_me], z_device(k))

    loop(depth - 1, lambda i: z_share(z_peer(i)).start())

    def z_got(i):
        k = z_peer(i)
        remote(full.at[z_span(k)], full.at[z_span(k)],
               s_zg.at[k], r_zg.at[k], z_device(k)).wait_recv()

    loop(depth - 1, z_got)
    mine = core * plane + p_me
    all_ref[mine] = full[0:tiles]

    def plane_share(k):
        return remote(all_ref.at[mine], all_ref.at[mine], s_pg.at[k], r_pg.at[p_me],
                      plane_device(k))

    def core_share(k):
        spot = all_ref.at[core * plane + k]
        return remote(spot, spot, s_cg.at[k], r_cg.at[k], partner)

    loop(plane - 1, lambda i: plane_share(plane_peer(i)).start())
    core_share(p_me).start()

    def plane_got(i):
        k = lax.rem(p_me + plane - 1 - i, plane)
        spot = all_ref.at[core * plane + k]
        remote(spot, spot, s_pg.at[k], r_pg.at[k], plane_device(k)).wait_recv()
        core_share(k).start()

    loop(plane - 1, plane_got)

    def core_got(k):
        spot = all_ref.at[(1 - core) * plane + k]
        remote(spot, spot, s_cg.at[k], r_cg.at[k], partner).wait_recv()

    loop(plane, core_got)

    def unpack(j):
        cols = pl.ds(pl.multiple_of(j * 128, 128), 128)
        for m in range(TILES):
            ref, base = (dt_ref, 0) if m < 4 else (b_ref, 4) if m < 12 else (c_ref, 12)
            a, b = tile(j * TILES + m)
            ref[8 * (m - base) : 8 * (m - base) + 8, cols] = all_ref[a, b]

    loop(G, unpack)
    a, b = tile(TILES * G)
    vec_ref[...] = all_ref[a, b]

    for r in range(2):
        loop(4, lambda q, r=r: swap(r, q).wait_send())
        loop(8, lambda g, r=r: hand(r, g).wait_send())
        loop(depth - 1, lambda i, r=r: to_chip(r, z_peer(i)).wait_send())
        loop(8 - per // 2, lambda i, r=r: to_owner(
            r, lax.rem((z_me + 1) * (per // 2) + i, 8)).wait_send())
        if halves == 2:
            pl.when(gives(r))(lambda r=r: across(r).wait_send())
    loop(plane, lambda k: core_copy(k).wait_send())
    loop(plane, lambda k: core_share(k).wait_send())
    loop(plane - 1, lambda i: plane_copy(plane_peer(i)).wait_send())
    loop(plane - 1, lambda i: plane_share(plane_peer(i)).wait_send())
    loop(depth - 1, lambda i: z_copy(z_peer(i)).wait_send())
    loop(depth - 1, lambda i: z_share(z_peer(i)).wait_send())


def deliver_kernel(*refs):
    sources, vec_ref = refs[0:5], refs[5]
    targets, rows, holds, sems_in, sems = refs[6:11], refs[11:14], refs[14:19], refs[19], refs[20]
    copies_in = [pltpu.make_async_copy(a, b, sems_in.at[n])
                 for n, (a, b) in enumerate(zip(sources, holds))]
    copies = [pltpu.make_async_copy(a, b, sems.at[n])
              for n, (a, b) in enumerate(zip(holds, targets))]
    for copy in copies_in:
        copy.start()
    for copy_in, copy in zip(copies_in, copies):
        copy_in.wait()
        copy.start()
    for n, row in enumerate(rows):
        row[...] = vec_ref[n : n + 1, 0:H]
    for copy in copies:
        copy.wait()


def sds(shape, dtype=F32):
    return jax.ShapeDtypeStruct(shape, dtype)


def on_device(sizes, sequence, n_blocks, w_dt, dt_bias, decay_rate, w_b, w_c, d_skip, cotangent):
    dps, ctxs = sizes
    chips = ctxs // 2
    halves = 2 if ctxs % 4 == 0 else 1
    depth = chips // halves
    plane = dps * halves
    tiles = -(-(TILES * G + 1) // (2 * plane))
    zt = -(-tiles // depth)
    per = PIECES // depth
    dma = pltpu.SemaphoreType.DMA

    def mem(*shape, dtype=F32):
        return pltpu.VMEM(shape, dtype)

    up, down = ROWS
    results = pl.pallas_call(
        functools.partial(kernel, halves, depth),
        out_shape=[sds((T, D), BF16), sds((T, D), BF16),
                   sds((H, D)), sds((N, D)), sds((N, D)), sds((8, 128))],
        in_specs=[VMEM, VMEM, SMEM] + [VMEM] * 6,
        out_specs=[VMEM] * 6,
        scratch_shapes=[
            mem(384, D, dtype=BF16), mem(384, D, dtype=BF16), mem(128, T),
            mem(T, D), mem(T, D), mem(T, T), mem(T, 128), mem(128, T), mem(T, 128),
            mem(T, T), mem(T, 384, dtype=BF16),
            mem(T, 128), mem(T, 128), mem(8, 128), mem(4, T, 128), mem(4, T, N),
            mem(2, PIECES, up, 128), mem(2, PIECES, down, 128),
            mem(PIECES, up, 128), mem(PIECES, down, 128),
            mem(PIECES, up, 128), mem(PIECES, down, 128),
            mem(depth, per, up, 128), mem(depth, per, down, 128),
            mem(depth, per, 64, 128), mem(depth, per, 64, 128),
            mem(depth, per, 64, 128), mem(depth, per, 64, 128),
            mem(PIECES, 128, 128), mem(2, PIECES, 128, 128),
            mem(2, per, 64, 128), mem(2, per, 64, 128),
            mem(2 * plane, tiles, 8, 128), mem(2 * plane, tiles, 8, 128),
            mem(plane, tiles, 8, 128), mem(plane, tiles, 8, 128), mem(plane, tiles, 8, 128),
            mem(depth * zt, 8, 128), mem(depth, zt, 8, 128), mem(depth * zt, 8, 128),
            dma((2, 4)), dma((2, 4)), dma((2, 8)), dma((2, 8)),
            dma((2, depth)), dma((2, depth)), dma((2,)), dma((2,)), dma((2, 8)), dma((2, 8)),
        ] + [dma((plane,))] * 4 + [dma((depth,))] * 4 + [dma((plane,))] * 4,
        compiler_params=pltpu.CompilerParams(
            vmem_limit_bytes=ALL, collective_id=0, has_side_effects=True),
    )(sequence[0], cotangent[0], n_blocks, w_dt.T, w_b.T, w_c.T,
      dt_bias[None], decay_rate[None], d_skip[None])

    anywhere = pl.BlockSpec(memory_space=pl.ANY)
    mixed, dseq, grad_dt, grad_b, grad_c, bias, rate, skip = pl.pallas_call(
        deliver_kernel,
        out_shape=[sds(a.shape, a.dtype) for a in results[0:5]] + [sds((1, H))] * 3,
        in_specs=[anywhere] * 5 + [VMEM],
        out_specs=[anywhere] * 5 + [VMEM] * 3,
        scratch_shapes=[mem(*a.shape, dtype=a.dtype) for a in results[0:5]] + [dma((5,)), dma((5,))],
        compiler_params=pltpu.CompilerParams(vmem_limit_bytes=ALL),
    )(*results)

    return (mixed[None], dseq[None], grad_dt.T, bias[0], rate[0],
            grad_b.T, grad_c.T, skip[0])


def solution(mesh):
    sizes = (mesh.shape["dp"], mesh.shape["ctx"])
    return jax.shard_map(
        functools.partial(on_device, sizes),
        mesh=mesh,
        in_specs=(
            P("dp", "ctx", None),
            P("dp", "ctx"),
            P(), P(), P(), P(), P(), P(),
            P("dp", "ctx", None),
        ),
        out_specs=(P("dp", "ctx", None), P("dp", "ctx", None), P(), P(), P(), P(), P(), P()),
        check_vma=False,
    )
```

```python
import functools

import jax
import jax.numpy as jnp
from jax import lax
from jax.experimental import pallas as pl
from jax.experimental.pallas import tpu as pltpu
from jax.sharding import PartitionSpec as P

F32 = jnp.float32
BF16 = jnp.bfloat16
BLOCK = 128
T = 256
D = 2048
H = 32
N = 64
G = 16
W = D // 256
MESH = pl.DeviceIdType.MESH
VMEM = pl.BlockSpec(memory_space=pltpu.VMEM)
SMEM = pl.BlockSpec(memory_space=pltpu.SMEM)
ALL = 62 * 1024 * 1024
PIECES = 16
ROWS = (72, 64)
TILES = 20
FAR = -1e30
EARLY, LATER = 10, 13


def iota(shape, axis):
    return lax.broadcasted_iota(jnp.int32, shape, axis)


def mat(a, b):
    return lax.dot_general(a, b, (((1,), (0,)), ((), ())), preferred_element_type=F32)


def mat_nt(a, b):
    return lax.dot_general(a, b, (((1,), (1,)), ((), ())), preferred_element_type=F32)


def split2(a):
    hi = a.astype(BF16)
    return hi, (a - hi.astype(F32)).astype(BF16)


def split3(a):
    hi = a.astype(BF16)
    rest = a - hi.astype(F32)
    mid = rest.astype(BF16)
    return hi, mid, (rest - mid.astype(F32)).astype(BF16)


def mat2(a, exact):
    hi, lo = split2(a)
    return mat(hi, exact) + mat(lo, exact)


def mat3(a, b):
    ah, al = split2(a)
    bh, bl = split2(b)
    return mat(ah, bh) + (mat(al, bh) + mat(ah, bl))


def mat3_nt(a, b):
    ah, al = split2(a)
    bh, bl = split2(b)
    return mat_nt(ah, bh) + (mat_nt(al, bh) + mat_nt(ah, bl))


def exact_left(zero_one, a):
    hi, mid, lo = split3(a)
    return mat(zero_one, hi) + (mat(zero_one, mid) + mat(zero_one, lo))


def exact_right(a, zero_one):
    hi, mid, lo = split3(a)
    return mat(hi, zero_one) + (mat(mid, zero_one) + mat(lo, zero_one))


def ones_where(condition):
    return jnp.where(condition, 1.0, 0.0).astype(BF16)


def backwards(size):
    return ones_where(iota((size, size), 0) + iota((size, size), 1) == size - 1)


def keep_column(nb_ref):
    first = 1.0 - nb_ref[0, 0].astype(F32)
    second = 1.0 - nb_ref[0, 1].astype(F32)
    return jnp.where(iota((T, 1), 0) < BLOCK, first, second)


def spread(first, second):
    rows = iota((128, 256), 0)
    cols = iota((128, 256), 1)
    head = jnp.where(cols < 128, 2 * first, 2 * second) + (cols % 128) // N
    return ones_where(rows == head), ones_where(rows == head + H)


def twice(a):
    return jnp.concatenate([a, a], axis=0)


def lanes2(a):
    return jnp.concatenate(split2(a), axis=1)


def inner_setup(c, bcf, bcr, sc, c3, dsc):
    row = iota((T, T), 0)
    col = iota((T, T), 1)
    sf = mat3_nt(bcf[:, N:], bcf[:, :N])
    sr = mat3_nt(bcr[:, N:], bcr[:, :N])
    sc[...] = jnp.where(row > col, sf, jnp.where(row < col, sr, 0.0))
    c3[...] = jnp.concatenate(split3(c), axis=1)
    dsc[...] = jnp.zeros((T, T), F32)


def inner_pair(i, x_ref, dy_ref, at_ref, sc, c3, y_ref, dx_ref, dsc, rs_ref, cs_ref, xi_ref):
    cols = pl.ds(pl.multiple_of(i * 128, 128), 128)
    xp = x_ref[:, cols]
    dp = dy_ref[:, cols]
    dpt = dp.astype(F32).T.astype(BF16)
    seg_rows = iota((128, 128), 0) // N + 2 * i
    seg_cols = iota((128, 128), 1)
    seg = ones_where((seg_cols < 2 * H) & (seg_cols % H == seg_rows))
    xi_ref[...] += mat2(dp.astype(F32) * xp.astype(F32), seg)
    lane = iota((1, 128), 1)
    row = iota((BLOCK, BLOCK), 0)
    col = iota((BLOCK, BLOCK), 1)
    low = row > col
    up = row < col
    lanes = iota((T, 128), 1)
    y = jnp.zeros((T, 128), F32)
    dut = []
    for k in range(2):
        h = 2 * i + k
        mask = ones_where((lane // N) == k)
        xm = xp * mask
        cross = mat_nt(dp * mask, xp)
        rows3 = iota((384, T), 0) % 128
        cols3 = iota((384, T), 1)
        sel = ones_where(rows3 == h + jnp.where(cols3 < 128, 0, H))
        cb = mat(c3[...], sel)
        af = at_ref[pl.ds(h, 1), :]
        ar = at_ref[pl.ds(H + h, 1), :]
        top = slice(0, BLOCK)
        bot = slice(BLOCK, T)

        def args(rows, columns):
            forward = cb[rows, 0:128] + af[:, columns]
            reverse = cb[rows, 128:256] + ar[:, columns]
            return forward, reverse

        e = {}
        for r in (top, bot):
            for q in (top, bot):
                f, b = args(r, q)
                if r is q:
                    arg = jnp.where(low, f, jnp.where(up, b, FAR))
                else:
                    arg = f if r is bot else b
                e[r is bot, q is bot] = jnp.exp(arg)
        kk = {}
        g = {}
        for r in (top, bot):
            for q in (top, bot):
                key = (r is bot, q is bot)
                kk[key] = sc[r, q] * e[key]
                xx = cross[r, q]
                g[key] = xx * kk[key]
                dsc[r, q] += xx * e[key]
        g0f = jnp.where(low, g[False, False], 0.0)
        g0r = g[False, False] - g0f
        g1f = jnp.where(low, g[True, True], 0.0)
        g1r = g[True, True] - g1f
        rf = jnp.concatenate(
            [jnp.sum(g0f, axis=1, keepdims=True),
             jnp.sum(g[True, False] + g1f, axis=1, keepdims=True)], axis=0)
        rr = jnp.concatenate(
            [jnp.sum(g0r + g[False, True], axis=1, keepdims=True),
             jnp.sum(g1r, axis=1, keepdims=True)], axis=0)
        rs_ref[...] = jnp.where(lanes == h, rf, jnp.where(lanes == H + h, rr, rs_ref[...]))
        cs_ref[pl.ds(h, 1), :] = jnp.concatenate(
            [jnp.sum(g0f + g[True, False], axis=0, keepdims=True),
             jnp.sum(g1f, axis=0, keepdims=True)], axis=1)
        cs_ref[pl.ds(H + h, 1), :] = jnp.concatenate(
            [jnp.sum(g0r, axis=0, keepdims=True),
             jnp.sum(g[False, True] + g1r, axis=0, keepdims=True)], axis=1)
        full = jnp.concatenate(
            [jnp.concatenate([kk[False, False], kk[False, True]], axis=1),
             jnp.concatenate([kk[True, False], kk[True, True]], axis=1)], axis=0)
        hi, lo = split2(full)
        y = y + mat(hi, xm) + mat(lo, xm)
        rows = dpt[N * k : N * (k + 1), :]
        dut.append(mat(rows, hi) + mat(rows, lo))
    y_ref[:, cols] = y
    dx_ref[:, cols] = jnp.concatenate(dut, axis=0).T


def kernel(halves, depth, x_ref, dy_ref, nb_ref, wdt_ref, wb_ref, wc_ref,
           bias_ref, rate_ref, skip_ref,
           mixed_ref, dseq_ref, dt_ref, b_ref, c_ref, vec_ref,
           whi, wlo, at_ref, y_in, dx, dsc, rs, cs, xi, sc, c3, rho, kap, omega, acc, accl,
           pack_up, pack_down, other_up, other_down, sums_up, sums_down, in_up, in_down,
           out_up, out_down, came_up, came_down, give, carried, whole, begin,
           grad, all_ref, from_core, held, from_plane, part, from_z, full,
           s_swap, r_swap, s_in, r_in, s_out, r_out, s_half, r_half, s_hand, r_hand,
           s_core, r_core, s_plane, r_plane, s_z, r_z, s_zg, r_zg, s_pg, r_pg, s_cg, r_cg):
    per = PIECES // depth
    pack, other = (pack_up, pack_down), (other_up, other_down)
    sums, inbox = (sums_up, sums_down), (in_up, in_down)
    outbox, came = (out_up, out_down), (came_up, came_down)
    plane = held.shape[0]
    tiles = held.shape[1]
    zt = from_z.shape[1]
    dp = lax.axis_index("dp")
    ctx = lax.axis_index("ctx")
    core = ctx % 2
    chip = ctx // 2
    z_me = chip % depth
    half_me = chip // depth
    p_me = dp * halves + half_me
    partner = (dp, ctx + 1 - 2 * core)

    def plane_device(k):
        return (k // halves, ((k % halves) * depth + z_me) * 2 + core)

    def plane_peer(i):
        return lax.rem(p_me + 1 + i, plane)

    def z_device(k):
        return (dp, (half_me * depth + k) * 2 + core)

    def z_peer(i):
        return lax.rem(z_me + 1 + i, depth)

    def remote(src, dst, send, recv, device):
        return pltpu.make_async_remote_copy(
            src_ref=src, dst_ref=dst, send_sem=send, recv_sem=recv,
            device_id=device, device_id_type=MESH,
        )

    def loop(count, body, start=0):
        def step(i, carry):
            body(i)
            return carry

        lax.fori_loop(start, count, step, 0)

    barrier = pltpu.get_barrier_semaphore()
    pl.semaphore_signal(barrier, inc=1, device_id=partner, device_id_type=MESH)
    loop(depth - 1, lambda i: pl.semaphore_signal(
        barrier, inc=1, device_id=z_device(z_peer(i)), device_id_type=MESH))
    loop(plane - 1, lambda i: pl.semaphore_signal(
        barrier, inc=1, device_id=plane_device(plane_peer(i)), device_id_type=MESH))

    flip = backwards(256)
    rev = backwards(H)
    both = ones_where((iota((H, 128), 1) == iota((H, 128), 0))
                      | (iota((H, 128), 1) + iota((H, 128), 0) == 2 * H - 1))
    bias, rate, skip = (
        exact_right(jnp.broadcast_to(ref[...], (8, H)), both)[0:1]
        for ref in (bias_ref, rate_ref, skip_ref)
    )

    def cut(i, carry):
        here = pl.ds(pl.multiple_of(i * 256, 256), 256)
        there = pl.ds(pl.multiple_of((W - 1 - i) * 256, 256), 256)
        raw = jnp.concatenate([wdt_ref[:, here], wb_ref[:, here], wc_ref[:, here]], axis=0)
        hi, lo = split2(raw)
        turned = mat(jnp.concatenate([hi, lo], axis=0), flip).astype(BF16)
        for ref, own, far in ((whi, hi, turned[0:160]), (wlo, lo, turned[160:320])):
            ref[0:H, here] = own[0:H]
            ref[128:256, here] = own[H:160]
            ref[H : 2 * H, there] = mat(rev, far[0:H]).astype(BF16)
            ref[256:384, there] = far[H:160]
            ref[2 * H : 128, here] = jnp.zeros((2 * H, 256), BF16)
        return carry

    lax.fori_loop(0, W, cut, 0, unroll=2)

    x = x_ref[...]
    proj = mat_nt(x, whi[...]) + mat_nt(x, wlo[...])
    lane = iota((T, 128), 1)
    row = iota((T, T), 0)
    col = iota((T, T), 1)
    keep = keep_column(nb_ref)
    z = proj[:, 0:128] + bias
    soft = jnp.maximum(z, 0.0) + jnp.log1p(jnp.exp(-jnp.abs(z)))
    step = jnp.where(lane < 2 * H, soft * keep, 0.0)
    fall = -step * rate
    c = jnp.where(
        lane < H,
        exact_left(ones_where(row >= col), fall),
        exact_left(ones_where(row <= col), fall),
    )
    last = jnp.where(lane[0:1] < H, c[T - 1 : T], c[0:1])
    at_ref[...] = jnp.where(step > 0.0, jnp.log(jnp.maximum(step, 1e-37)) - c, FAR).T
    bcf = proj[:, 128:256]
    bcr = proj[:, 256:384]
    e2 = lanes2(jnp.exp(c))
    tail2 = lanes2(jnp.exp(last - c) * step)
    decay8 = jnp.broadcast_to(jnp.exp(last), (8, 128))
    tf_hi, tf_lo = split2(bcf.T)
    tr_hi, tr_lo = split2(bcr.T)

    lefts = [
        jnp.concatenate([hi[span], lo[span]], axis=0)
        for hi, lo, span in (
            (tf_hi, tf_lo, slice(0, N)),
            (tr_hi, tr_lo, slice(N, 2 * N)),
            (tr_hi, tr_lo, slice(0, N)),
            (tf_hi, tf_lo, slice(N, 2 * N)),
        )
    ]
    first = (core == 0, core == 1)

    def block(i):
        return lax.rem(i + z_me * per // 4, 4)

    def swap(r, q):
        spot = pl.ds(4 * q, 4)
        return remote(pack[r].at[1 - core, spot], other[r].at[spot],
                      s_swap.at[r, q], r_swap.at[r, q], partner)

    def slot(k, g):
        return k * (per // 2) + g % (per // 2)

    def to_owner(r, g):
        return remote(sums[r].at[pl.ds(2 * g, 2), pl.ds(0, ROWS[r])],
                      inbox[r].at[z_me, pl.ds(2 * g % per, 2)],
                      s_in.at[r, g], r_in.at[r, slot(z_me, g)], z_device(2 * g // per))

    def local_states(r, half, q):
        i = 4 * half + q
        cols = pl.ds(pl.multiple_of(i * 256, 256), 256)
        sel_f, sel_r = spread(2 * i, 2 * i + 1)
        two_f, two_r = twice(sel_f), twice(sel_r)
        xj = x_ref[:, cols].astype(F32)
        dj = dy_ref[:, cols].astype(F32)
        if r == 0:
            rights = mat(tail2, two_f) * xj, mat(e2, two_r) * dj
            drops = jnp.where(iota((8, 256), 0) == 0,
                              exact_right(decay8, sel_f), exact_right(decay8, sel_r))
        else:
            rights = mat(tail2, two_r) * xj, mat(e2, two_f) * dj
        for s in range(2):
            left = lefts[2 * r + s]
            hi, lo = split2(rights[s])
            wide = mat(left, hi)
            got = wide[0:N] + wide[N : 2 * N] + mat(left[0:N], lo)
            for g in range(2):
                lanes = slice(128 * g, 128 * g + 128)
                for h in range(2):
                    p = 4 * q + 2 * g + h
                    pack[r][half, p, 32 * s : 32 * s + 32, :] = got[32 * h : 32 * h + 32, lanes]
                    if r == 0 and s == 0:
                        pack[r][half, p, 64:72, :] = drops[:, lanes]

    def drop_rows(r, p):
        mine = pack_up[core, p, 64:72, :]
        theirs = other_up[p, 64:72, :]
        order = (0, 1) if r == 0 else (1, 0)
        return [(mine[n : n + 1], theirs[n : n + 1]) for n in order]

    def add_up(r, q):
        swap(r, q).wait_recv()
        for n in range(2):
            g = 2 * q + n
            own = 2 * g // per == z_me
            both_pieces = []
            for p in (2 * g, 2 * g + 1):
                drops = drop_rows(r, p)
                out = []
                for s in range(2):
                    rows = slice(32 * s, 32 * s + 32)
                    dm, dt = drops[s]
                    mine = pack[r][core, p, rows, :]
                    theirs = other[r][p, rows, :]
                    out.append(jnp.where(first[r], dt * mine + theirs, dm * theirs + mine))
                if r == 0:
                    out.append(pack_up[core, p, 64:72, :] * other_up[p, 64:72, :])
                both_pieces.append(jnp.concatenate(out, axis=0))

            @pl.when(own)
            def _():
                for h in range(2):
                    inbox[r][z_me, 2 * g % per + h] = both_pieces[h]

            @pl.when(jnp.logical_not(own))
            def _():
                for h in range(2):
                    sums[r][2 * g + h] = both_pieces[h]
                to_owner(r, g).start()

    pl.semaphore_wait(barrier, plane + depth - 1)
    for r in range(2):
        def states(i, r=r):
            @pl.when(i < 4)
            def _():
                q = block(i)
                local_states(r, 1 - core, q)
                swap(r, q).start()
                local_states(r, core, q)

            @pl.when(i > 0)
            def _():
                add_up(r, block(i - 1))

        loop(5, states)

    inner_setup(c, bcf, bcr, sc, c3, dsc)
    rs[...] = jnp.zeros((T, 128), F32)
    cs[...] = jnp.zeros((128, T), F32)
    xi[...] = jnp.zeros((T, 128), F32)
    for ref in (rho, kap, omega, acc, accl):
        ref[...] = jnp.zeros(ref.shape, F32)

    def inner(i):
        inner_pair(i, x_ref, dy_ref, at_ref, sc, c3, y_in, dx, dsc, rs, cs, xi)

    def to_chip(r, k):
        return remote(outbox[r].at[k], came[r].at[z_me],
                      s_out.at[r, k], r_out.at[r, z_me], z_device(k))

    def across(r):
        return remote(whole.at[r], begin.at[r], s_half.at[r], r_half.at[r],
                      (dp, ((1 - half_me) * depth + z_me) * 2 + core))

    def scan(r):
        def piece(u):
            def turn(i, run):
                k = i if r == 0 else depth - 1 - i
                outbox[r][k, u] = run
                drop = in_up[k, u, 64:72, :]
                one, two = (drop[0:1], drop[1:2]) if r == 0 else (drop[1:2], drop[0:1])
                return (jnp.concatenate([one * run[0:32], two * run[32:64]], axis=0)
                        + inbox[r][k, u, 0:64, :])

            whole[r, u] = lax.fori_loop(0, depth, turn, begin[r, u])

        loop(per, piece)

    def scatter(r):
        loop(depth - 1, lambda i: to_chip(r, z_peer(i)).start())
        came[r][z_me] = outbox[r][z_me]

    def gives(r):
        return half_me == (0 if r == 0 else halves - 1)

    def collect(r):
        def arrived(i):
            k = z_peer(i)
            for n in range(per // 2):
                g = k * (per // 2) + n
                remote(sums[r].at[pl.ds(2 * g, 2), pl.ds(0, ROWS[r])],
                       inbox[r].at[k, pl.ds(2 * n, 2)],
                       s_in.at[r, g], r_in.at[r, g], z_device(k)).wait_recv()

        loop(depth - 1, arrived)

        @pl.when(gives(r))
        def _():
            begin[r] = jnp.zeros((per, 64, 128), F32)
            scan(r)
            if halves == 2:
                across(r).start()
            scatter(r)

    def finish(r):
        @pl.when(jnp.logical_not(gives(r)))
        def _():
            across(r).wait_recv()
            scan(r)
            scatter(r)

    loop(EARLY, inner)
    collect(0)
    loop(LATER, inner, EARLY)
    finish(0)
    loop(G, inner, LATER)
    collect(1)
    finish(1)

    sig_f = jnp.sum(bcf[:, :N] * bcf[:, N:], axis=1, keepdims=True)
    sig_r = jnp.sum(bcr[:, :N] * bcr[:, N:], axis=1, keepdims=True)
    sigma = jnp.where(lane < H, sig_f, jnp.where(lane < 2 * H, sig_r, 0.0))
    coef3 = jnp.concatenate(split3(sigma * step + skip), axis=1)

    def left3(a):
        hi, lo = split2(a)
        return jnp.concatenate([hi, lo, hi], axis=1)

    l_bf, l_cf = left3(bcf[:, :N]), left3(bcf[:, N:])
    l_br, l_cr = left3(bcr[:, :N]), left3(bcr[:, N:])

    def group_of(i):
        return lax.rem(z_me * per // 2 + i, 8)

    def hand(r, g):
        spot = pl.ds(2 * g, 2)
        rows = pl.ds(64 * r, 64)
        return remote(give.at[spot, rows], carried.at[core, spot, rows],
                      s_hand.at[r, g], r_hand.at[r, g], partner)

    def receive(r, i):
        g = group_of(i)
        k = 2 * g // per

        @pl.when((k != z_me) & (2 * g % per == 0))
        def _():
            remote(outbox[r].at[k], came[r].at[k], s_out.at[r, k], r_out.at[r, k],
                   z_device(k)).wait_recv()

        for p in (2 * g, 2 * g + 1):
            drops = drop_rows(r, p)
            for s in range(2):
                rows = slice(32 * s, 32 * s + 32)
                to = slice(64 * r + 32 * s, 64 * r + 32 * s + 32)
                dm, dt = drops[s]
                got = came[r][k, p % per, rows, :]
                mine = pack[r][core, p, rows, :]
                theirs = other[r][p, rows, :]
                carried[core, p, to, :] = jnp.where(first[r], got, dt * got + theirs)
                give[p, to, :] = jnp.where(first[r], dm * got + mine, got)
        hand(r, g).start()

    def work(r, i):
        g = group_of(i)
        spot = pl.ds(2 * g, 2)
        span = pl.ds(64 * r, 64)
        remote(give.at[spot, span], carried.at[1 - core, spot, span],
               s_hand.at[r, g], r_hand.at[r, g], partner).wait_recv()
        groups = (8 * core + g, 8 * (1 - core) + g)
        places = [pl.ds(pl.multiple_of(j * 128, 128), 128) for j in groups]

        def wide(ref):
            return jnp.concatenate([ref[:, p] for p in places], axis=1)

        def state(s):
            rows = slice(32 * s, 32 * s + 32)
            return jnp.concatenate(
                [jnp.concatenate([carried[h, 2 * g, rows, :], carried[h, 2 * g + 1, rows, :]], axis=0)
                 for h in (core, 1 - core)], axis=1)

        now, adj = state(2 * r), state(2 * r + 1)
        sel = spread(*groups)
        sel_s, sel_a = sel[r], sel[1 - r]
        e = mat(e2, twice(sel_s))
        t = mat(tail2, twice(sel_a))
        xj = wide(x_ref).astype(F32)
        dj = wide(dy_ref).astype(F32)
        w = t * xj
        cut_s, cut_a = split2(now), split2(adj)

        def times(left, cut):
            return mat(left, jnp.concatenate([cut[0], cut[0], cut[1]], axis=0))

        y = e * times((l_cf, l_cr)[r], cut_s)
        v = times((l_br, l_bf)[r], cut_a)
        out = wide(y_in) + y
        more = wide(dx) + t * v
        if r == 0:
            one = sel[0] + sel[1]
            coef = mat(coef3, jnp.concatenate([one, one, one], axis=0))
            out = out + coef * xj
            more = more + coef * dj
        for n, p in enumerate(places):
            part_out = out[:, 128 * n : 128 * n + 128]
            if r == 0:
                y_in[:, p] = part_out
            else:
                mixed_ref[:, p] = part_out.astype(BF16)
            dx[:, p] = more[:, 128 * n : 128 * n + 128]
        back = [a.astype(F32).T.astype(BF16) for a in sel]
        rho[...] += mat2(dj * y, back[r])
        kap[...] += mat2(w * v, back[1 - r])
        if r == 1:
            in_f = jnp.sum(state(0) * adj, axis=0, keepdims=True)
            in_r = jnp.sum(now * state(1), axis=0, keepdims=True)
            omega[...] += (exact_right(jnp.broadcast_to(in_f, (8, 256)), back[0])
                           + exact_right(jnp.broadcast_to(in_r, (8, 256)), back[1]))
        for n, left, cut in ((r, e * dj, cut_s), (3 - r, w, cut_a)):
            hi, lo = split2(left)
            acc[n] += mat_nt(hi, jnp.concatenate(cut, axis=0))
            accl[n] += mat_nt(lo, cut[0])

    ksi = xi[...]
    diag = step * ksi
    ds_f = jnp.sum(jnp.where(lane < H, diag, 0.0), axis=1, keepdims=True)
    ds_r = jnp.sum(jnp.where((lane >= H) & (lane < 2 * H), diag, 0.0), axis=1, keepdims=True)
    mixing = dsc[...]
    turned = mixing.T
    eq = row == col
    m_f = jnp.where(eq, ds_f, jnp.where(row > col, mixing, 0.0))
    m_r = jnp.where(eq, ds_r, jnp.where(row < col, mixing, 0.0))
    mt_f = jnp.where(eq, ds_f, jnp.where(row < col, turned, 0.0))
    mt_r = jnp.where(eq, ds_r, jnp.where(row > col, turned, 0.0))
    own_bf, own_cf = mat3(mt_f, bcf[:, N:]), mat3(m_f, bcf[:, :N])
    own_br, own_cr = mat3(mt_r, bcr[:, N:]), mat3(m_r, bcr[:, :N])

    for r in range(2):
        def arrive(i, r=r):
            @pl.when(i < 8)
            def _():
                receive(r, i)

            @pl.when(i > 0)
            def _():
                work(r, i - 1)

        loop(9, arrive)

    def total(n):
        a = acc[n]
        return a[:, :N] + a[:, N:] + accl[n]

    colsum = cs[...].T
    kappa = kap[...]
    through = rs[...] - colsum + rho[...]
    d_fall = jnp.where(
        lane < H,
        exact_left(ones_where(row <= col), through) + exact_left(ones_where(row > col), kappa),
        exact_left(ones_where(row >= col), through) + exact_left(ones_where(row < col), kappa),
    ) + omega[0:1, :] * jnp.exp(last)
    small = jnp.exp(-jnp.abs(z))
    soft = jnp.maximum(z, 0.0) + jnp.log1p(small)
    sigmoid = jnp.where(z >= 0.0, 1.0, small) / (1.0 + small)
    ratio = jnp.where(z < -30.0, 1.0, sigmoid / jnp.maximum(soft, 1e-30))
    straight = colsum + kappa + sigma * diag
    dz = straight * ratio - rate * d_fall * sigmoid * keep
    dz = jnp.where(lane < 2 * H, dz, 0.0)

    d_bcf = jnp.concatenate([total(2) + own_bf, total(0) + own_cf], axis=1)
    d_bcr = jnp.concatenate([total(3) + own_br, total(1) + own_cr], axis=1)
    dproj = jnp.concatenate([dz, d_bcf, d_bcr], axis=1)
    p_hi, p_lo = split2(dproj)
    p_cat = jnp.concatenate([p_hi, p_lo, p_hi], axis=1)

    r128 = iota((128, 128), 0)
    c128 = iota((128, 128), 1)
    fold = ones_where(((r128 < H) & (r128 == c128))
                      | ((r128 >= H) & (r128 < 2 * H) & (r128 + c128 == 2 * H - 1)))
    vectors = jnp.concatenate(
        [jnp.sum(dz, axis=0, keepdims=True),
         -jnp.sum(step * d_fall, axis=0, keepdims=True),
         jnp.sum(ksi, axis=0, keepdims=True),
         jnp.zeros((5, 128), F32)], axis=0)
    dz_t = dz.T
    f_t = jnp.concatenate([dz_t[0:H], d_bcf.T], axis=0)
    r_hi, r_lo = split2(jnp.concatenate([dz_t[H : 2 * H], d_bcr.T], axis=0))
    f_hi, f_lo = split2(f_t)

    def ordered(a):
        return jnp.concatenate([mat(rev, a[0:H]).astype(BF16), a[H:]], axis=0)

    left = jnp.concatenate(
        [jnp.concatenate([f_hi, ordered(r_hi)], axis=1),
         jnp.concatenate([f_lo, ordered(r_lo)], axis=1)], axis=0)

    def tile(n):
        return (n // tiles, n % tiles)

    def weights(j):
        i = lax.rem(j + (W // 2) * (1 - core), W)
        cols = pl.ds(pl.multiple_of(i * 256, 256), 256)
        far = pl.ds(pl.multiple_of((W - 1 - i) * 256, 256), 256)
        right = jnp.concatenate(
            [x_ref[:, cols], mat(x_ref[:, far], flip).astype(BF16)], axis=0)
        got = mat(left, right)
        got = got[0:160] + got[160:320]
        for n in range(2):
            for m in range(TILES):
                a, b = tile((2 * i + n) * TILES + m)
                grad[a, b] = got[8 * m : 8 * m + 8, 128 * n : 128 * n + 128]

    def blank(n):
        a, b = tile(n)
        grad[a, b] = jnp.zeros((8, 128), F32)

    loop(2 * plane * tiles, blank, TILES * G + 1)
    a, b = tile(TILES * G)
    grad[a, b] = exact_right(vectors, fold)

    def core_copy(k):
        return remote(grad.at[(1 - core) * plane + k], from_core.at[k],
                      s_core.at[k], r_core.at[k], partner)

    def plane_copy(k):
        return remote(held.at[k], from_plane.at[p_me], s_plane.at[k], r_plane.at[p_me],
                      plane_device(k))

    loop(W // 2 + 1, weights)
    loop(plane, lambda i: core_copy(plane_peer(i)).start())
    loop(W, weights, W // 2 + 1)

    def add_core(i):
        k = plane_peer(i)
        core_copy(k).wait_recv()
        held[k] = grad[core * plane + k] + from_core[k]

    def forward(i):
        add_core(i)
        plane_copy(plane_peer(i)).start()

    loop(plane - 1, forward)
    add_core(plane - 1)

    def sequence(i):
        cols = pl.ds(pl.multiple_of(i * 256, 256), 256)
        w_hi = whi[:, cols]
        w_cat = jnp.concatenate([w_hi, w_hi, wlo[:, cols]], axis=0)
        dseq_ref[:, cols] = (dx[:, cols] + mat(p_cat, w_cat)).astype(BF16)

    loop(W, sequence)
    part[...] = jnp.zeros(part.shape, F32)
    part[0:tiles] = held[p_me]

    def add_plane(i):
        k = lax.rem(p_me + plane - 1 - i, plane)
        remote(held.at[k], from_plane.at[k], s_plane.at[k], r_plane.at[k],
               plane_device(k)).wait_recv()
        part[0:tiles] += from_plane[k]

    loop(plane - 1, add_plane)

    def z_span(k):
        return pl.ds(k * zt, zt)

    def z_copy(k):
        return remote(part.at[z_span(k)], from_z.at[z_me], s_z.at[k], r_z.at[z_me], z_device(k))

    loop(depth - 1, lambda i: z_copy(z_peer(i)).start())
    full[z_span(z_me)] = part[z_span(z_me)]

    def add_z(i):
        k = z_peer(i)
        remote(part.at[z_span(k)], from_z.at[k], s_z.at[k], r_z.at[k], z_device(k)).wait_recv()
        full[z_span(z_me)] += from_z[k]

    loop(depth - 1, add_z)

    def z_share(k):
        return remote(full.at[z_span(z_me)], full.at[z_span(z_me)],
                      s_zg.at[k], r_zg.at[z_me], z_device(k))

    loop(depth - 1, lambda i: z_share(z_peer(i)).start())

    def z_got(i):
        k = z_peer(i)
        remote(full.at[z_span(k)], full.at[z_span(k)],
               s_zg.at[k], r_zg.at[k], z_device(k)).wait_recv()

    loop(depth - 1, z_got)
    mine = core * plane + p_me
    all_ref[mine] = full[0:tiles]

    def plane_share(k):
        return remote(all_ref.at[mine], all_ref.at[mine], s_pg.at[k], r_pg.at[p_me],
                      plane_device(k))

    def core_share(k):
        spot = all_ref.at[core * plane + k]
        return remote(spot, spot, s_cg.at[k], r_cg.at[k], partner)

    loop(plane - 1, lambda i: plane_share(plane_peer(i)).start())
    core_share(p_me).start()

    def plane_got(i):
        k = lax.rem(p_me + plane - 1 - i, plane)
        spot = all_ref.at[core * plane + k]
        remote(spot, spot, s_pg.at[k], r_pg.at[k], plane_device(k)).wait_recv()
        core_share(k).start()

    loop(plane - 1, plane_got)

    def core_got(k):
        spot = all_ref.at[(1 - core) * plane + k]
        remote(spot, spot, s_cg.at[k], r_cg.at[k], partner).wait_recv()

    loop(plane, core_got)

    def unpack(j):
        cols = pl.ds(pl.multiple_of(j * 128, 128), 128)
        for m in range(TILES):
            ref, base = (dt_ref, 0) if m < 4 else (b_ref, 4) if m < 12 else (c_ref, 12)
            a, b = tile(j * TILES + m)
            ref[8 * (m - base) : 8 * (m - base) + 8, cols] = all_ref[a, b]

    loop(G, unpack)
    a, b = tile(TILES * G)
    vec_ref[...] = all_ref[a, b]

    for r in range(2):
        loop(4, lambda q, r=r: swap(r, q).wait_send())
        loop(8, lambda g, r=r: hand(r, g).wait_send())
        loop(depth - 1, lambda i, r=r: to_chip(r, z_peer(i)).wait_send())
        loop(8 - per // 2, lambda i, r=r: to_owner(
            r, lax.rem((z_me + 1) * (per // 2) + i, 8)).wait_send())
        if halves == 2:
            pl.when(gives(r))(lambda r=r: across(r).wait_send())
    loop(plane, lambda k: core_copy(k).wait_send())
    loop(plane, lambda k: core_share(k).wait_send())
    loop(plane - 1, lambda i: plane_copy(plane_peer(i)).wait_send())
    loop(plane - 1, lambda i: plane_share(plane_peer(i)).wait_send())
    loop(depth - 1, lambda i: z_copy(z_peer(i)).wait_send())
    loop(depth - 1, lambda i: z_share(z_peer(i)).wait_send())


def deliver_kernel(*refs):
    sources, vec_ref = refs[0:5], refs[5]
    targets, rows, holds, sems_in, sems = refs[6:11], refs[11:14], refs[14:19], refs[19], refs[20]
    copies_in = [pltpu.make_async_copy(a, b, sems_in.at[n])
                 for n, (a, b) in enumerate(zip(sources, holds))]
    copies = [pltpu.make_async_copy(a, b, sems.at[n])
              for n, (a, b) in enumerate(zip(holds, targets))]
    for copy in copies_in:
        copy.start()
    for copy_in, copy in zip(copies_in, copies):
        copy_in.wait()
        copy.start()
    for n, row in enumerate(rows):
        row[...] = vec_ref[n : n + 1, 0:H]
    for copy in copies:
        copy.wait()


def sds(shape, dtype=F32):
    return jax.ShapeDtypeStruct(shape, dtype)


def on_device(sizes, sequence, n_blocks, w_dt, dt_bias, decay_rate, w_b, w_c, d_skip, cotangent):
    dps, ctxs = sizes
    chips = ctxs // 2
    halves = 2 if ctxs % 4 == 0 else 1
    depth = chips // halves
    plane = dps * halves
    tiles = -(-(TILES * G + 1) // (2 * plane))
    zt = -(-tiles // depth)
    per = PIECES // depth
    dma = pltpu.SemaphoreType.DMA

    def mem(*shape, dtype=F32):
        return pltpu.VMEM(shape, dtype)

    up, down = ROWS
    results = pl.pallas_call(
        functools.partial(kernel, halves, depth),
        out_shape=[sds((T, D), BF16), sds((T, D), BF16),
                   sds((H, D)), sds((N, D)), sds((N, D)), sds((8, 128))],
        in_specs=[VMEM, VMEM, SMEM] + [VMEM] * 6,
        out_specs=[VMEM] * 6,
        scratch_shapes=[
            mem(384, D, dtype=BF16), mem(384, D, dtype=BF16), mem(128, T),
            mem(T, D), mem(T, D), mem(T, T), mem(T, 128), mem(128, T), mem(T, 128),
            mem(T, T), mem(T, 384, dtype=BF16),
            mem(T, 128), mem(T, 128), mem(8, 128), mem(4, T, 128), mem(4, T, N),
            mem(2, PIECES, up, 128), mem(2, PIECES, down, 128),
            mem(PIECES, up, 128), mem(PIECES, down, 128),
            mem(PIECES, up, 128), mem(PIECES, down, 128),
            mem(depth, per, up, 128), mem(depth, per, down, 128),
            mem(depth, per, 64, 128), mem(depth, per, 64, 128),
            mem(depth, per, 64, 128), mem(depth, per, 64, 128),
            mem(PIECES, 128, 128), mem(2, PIECES, 128, 128),
            mem(2, per, 64, 128), mem(2, per, 64, 128),
            mem(2 * plane, tiles, 8, 128), mem(2 * plane, tiles, 8, 128),
            mem(plane, tiles, 8, 128), mem(plane, tiles, 8, 128), mem(plane, tiles, 8, 128),
            mem(depth * zt, 8, 128), mem(depth, zt, 8, 128), mem(depth * zt, 8, 128),
            dma((2, 4)), dma((2, 4)), dma((2, 8)), dma((2, 8)),
            dma((2, depth)), dma((2, depth)), dma((2,)), dma((2,)), dma((2, 8)), dma((2, 8)),
        ] + [dma((plane,))] * 4 + [dma((depth,))] * 4 + [dma((plane,))] * 4,
        compiler_params=pltpu.CompilerParams(
            vmem_limit_bytes=ALL, collective_id=0, has_side_effects=True),
    )(sequence[0], cotangent[0], n_blocks, w_dt.T, w_b.T, w_c.T,
      dt_bias[None], decay_rate[None], d_skip[None])

    anywhere = pl.BlockSpec(memory_space=pl.ANY)
    mixed, dseq, grad_dt, grad_b, grad_c, bias, rate, skip = pl.pallas_call(
        deliver_kernel,
        out_shape=[sds(a.shape, a.dtype) for a in results[0:5]] + [sds((1, H))] * 3,
        in_specs=[anywhere] * 5 + [VMEM],
        out_specs=[anywhere] * 5 + [VMEM] * 3,
        scratch_shapes=[mem(*a.shape, dtype=a.dtype) for a in results[0:5]] + [dma((5,)), dma((5,))],
        compiler_params=pltpu.CompilerParams(vmem_limit_bytes=ALL),
    )(*results)

    return (mixed[None], dseq[None], grad_dt.T, bias[0], rate[0],
            grad_b.T, grad_c.T, skip[0])


def solution(mesh):
    sizes = (mesh.shape["dp"], mesh.shape["ctx"])
    return jax.shard_map(
        functools.partial(on_device, sizes),
        mesh=mesh,
        in_specs=(
            P("dp", "ctx", None),
            P("dp", "ctx"),
            P(), P(), P(), P(), P(), P(),
            P("dp", "ctx", None),
        ),
        out_specs=(P("dp", "ctx", None), P("dp", "ctx", None), P(), P(), P(), P(), P(), P()),
        check_vma=False,
    )
```
